32 devices in a mesh: groups: 2 (over x), ctx: 16 (over z, y, core).
Axes of the slice: x: 2, y: 2, z: 4, core: 2. Of those that a mesh axis runs over, the one named last changes fastest.
Arguments:
- queries: bfloat16 [4096, 4096], P(('groups', 'ctx')), parts along dimension 0, may hold values from -6 to 6
- key_input: bfloat16 [4096, 4096], P(('groups', 'ctx')), parts along dimension 0, may hold values from -6 to 6
- value_input: bfloat16 [4096, 4096], P(('groups', 'ctx')), parts along dimension 0, may hold values from -6 to 6
- log_decay: float32 [4096, 32], P(('groups', 'ctx')), parts along dimension 0, may hold values from -2.5 to 0
- conv_weight: float32 [4, 4096], replicated, may hold values from -3 to 3
- norm_gain: float32 [4096], replicated, may hold values from 0.1 to 1.9
Outputs:
- mixed_out: bfloat16 [4096, 4096], P(('groups', 'ctx')), parts along dimension 0
The draws below stay inside these ranges and needn't reach their ends.
There are 2 independent parts, one for each index of `groups`. The reference program is written for one: setup_inputs(seed, part) draws one part's arguments, and reference() takes and returns one part's arrays. A program takes and returns all parts, laid end to end along the dimension named above; an argument that names none is the same for every part. Nothing has to cross between parts.
All inputs are finite; a program needn't handle non-finite values.
Results may differ from the reference program's by a relative error of at most 0.0066.
Values may be sent and summed in bfloat16 or wider, within the bound.
A program may use at most 320 MiB of HBM per device.

```python
import math
import jax
import jax.numpy as jnp
from jax import lax

SHARD_HEADS = 32
HEAD_DIM = 128
KERNEL = 4
TOK_DEV = 128
WIDTH = 4096
SEQUENCE_TOKENS = 2048


def draw_log_decay(key, part):
    complete_keys = jax.random.split(jax.random.fold_in(key, 17), 10)
    rapid_fraction = 0.375
    surge_ratio = 0.375
    head_selection = jax.random.uniform(complete_keys[0], (SHARD_HEADS,))
    is_fast = head_selection < rapid_fraction
    surge_flag = jnp.logical_and(head_selection >= rapid_fraction, head_selection < rapid_fraction + surge_ratio)
    fast_rate = jnp.exp(jax.random.uniform(complete_keys[1], (SHARD_HEADS,), jnp.float32, math.log(1.0 / 50.0), math.log(1.0 / 30.0)))
    slow_rate = -math.log(0.95) / SEQUENCE_TOKENS * jnp.exp(jax.random.uniform(complete_keys[2], (SHARD_HEADS,), jnp.float32, math.log(0.3), 0.0))
    head_rate = jnp.where(is_fast, fast_rate, slow_rate)
    factor = jnp.exp(jax.random.uniform(complete_keys[3], (SEQUENCE_TOKENS, SHARD_HEADS), jnp.float32, math.log(0.5), math.log(2.0)))
    baseline_fraction = -head_rate[None, :] * factor
    spike_position = jax.random.randint(complete_keys[4], (3, SHARD_HEADS), 0, SEQUENCE_TOKENS)
    spike_loss = jax.random.uniform(complete_keys[5], (3, SHARD_HEADS), jnp.float32, 0.2, 0.5)
    token_location = jnp.arange(SEQUENCE_TOKENS)[:, None, None]
    marked_tokens = token_location == spike_position[None]
    peak_fraction = jnp.sum(jnp.where(marked_tokens, jnp.log1p(-spike_loss)[None], 0.0), axis=1)
    block_ordinal = SEQUENCE_TOKENS // TOK_DEV
    surge_count = max(block_ordinal // 8, 2)
    surge_interval = SEQUENCE_TOKENS // surge_count
    surge_offset = jax.random.randint(complete_keys[6], (surge_count, SHARD_HEADS), 0, surge_interval - 2)
    surge_begin = jnp.arange(surge_count)[:, None] * surge_interval + surge_offset
    heavy_selection = jax.random.uniform(complete_keys[7], (surge_count, SHARD_HEADS)) < 0.5
    heavy_total = jax.random.uniform(complete_keys[8], (surge_count, SHARD_HEADS), jnp.float32, -5.0, -4.7)
    gentle_total = jax.random.uniform(complete_keys[9], (surge_count, SHARD_HEADS), jnp.float32, -3.5, -1.2)
    surge_tokens_total = jnp.where(heavy_selection, heavy_total, gentle_total)
    within_surge = jnp.logical_and(token_location >= surge_begin[None], token_location < surge_begin[None] + 3)
    surge_fraction = jnp.sum(jnp.where(within_surge, (surge_tokens_total / 3.0)[None], 0.0), axis=1)
    surge_fraction = jnp.where(surge_flag[None, :], surge_fraction, 0.0)
    merged_result = baseline_fraction + peak_fraction + surge_fraction
    return jnp.maximum(merged_result, -2.5).astype(jnp.float32)


def block_levels(rng, shape, shards, low, largest):
    loudness = 1.0
    for axis_at, parts in shards:
        steps = jax.random.uniform(jax.random.fold_in(jax.random.fold_in(rng, 6), axis_at), (parts,), jnp.float32, low / len(shards), largest / len(shards))
        loudness = loudness * jnp.repeat(jnp.exp(steps), shape[axis_at] // parts).reshape((-1,) + (1,) * (len(shape) - 1 - axis_at))
    return loudness


def gaussian(rng, extent, scale, reach, pieces=(), kind=jnp.bfloat16):
    array = jax.random.normal(rng, extent, jnp.float32) * scale
    if len(pieces) > 0:
        array = block_levels(rng, extent, pieces, -0.22, 0.18) * array
    return jnp.clip(array, min=-reach, max=reach).astype(kind)


def setup_inputs(seed: int = 0, part: int = 0) -> dict:
    seeds = jax.random.split(jax.random.key(seed), 7)
    part_keys = jax.random.split(jax.random.fold_in(seeds[6], part), 7)
    queries = gaussian(part_keys[0], (SEQUENCE_TOKENS, WIDTH), 1.0, 6.0, ((0, 16),))
    key_input = gaussian(part_keys[1], (SEQUENCE_TOKENS, WIDTH), 1.0, 6.0, ((0, 16),))
    value_input = gaussian(part_keys[2], (SEQUENCE_TOKENS, WIDTH), 1.0, 6.0, ((0, 16),))
    log_decay = draw_log_decay(jax.random.fold_in(jax.random.fold_in(seeds[6], part), 71), part)
    conv_weight = gaussian(seeds[4], (KERNEL, WIDTH), 0.6, 3.0, (), jnp.float32)
    norm_gain = jnp.clip(1.0 + 0.18 * jax.random.normal(seeds[5], (WIDTH,), jnp.float32), 0.1, 1.9)
    return dict(queries=queries, key_input=key_input, value_input=value_input, log_decay=log_decay, conv_weight=conv_weight, norm_gain=norm_gain)


def reference(queries, key_input, value_input, log_decay, conv_weight, norm_gain):
    block_count = SEQUENCE_TOKENS // TOK_DEV
    taps = KERNEL
    query_blocks = queries.reshape(block_count, TOK_DEV, SHARD_HEADS, HEAD_DIM)
    key_blocks = key_input.reshape(block_count, TOK_DEV, WIDTH)
    value_blocks = value_input.reshape(block_count, TOK_DEV, SHARD_HEADS, HEAD_DIM)
    decay_blocks = log_decay.reshape(block_count, TOK_DEV, SHARD_HEADS)
    gain_heads = norm_gain.reshape(SHARD_HEADS, HEAD_DIM)
    causal = jnp.arange(TOK_DEV)[:, None] >= jnp.arange(TOK_DEV)[None, :]

    def one_block(carry, inputs):
        prefix, key_tail = carry
        query_blk, key_raw, value_blk, decay_blk = inputs
        extended = jnp.concatenate([key_tail, key_raw], 0)
        conv_sum = jnp.zeros((TOK_DEV, WIDTH), jnp.float32)
        for offset in range(taps):
            start = taps - 1 - offset
            conv_sum = conv_sum + conv_weight[offset][None, :] * extended[start:start + TOK_DEV].astype(jnp.float32)
        key_conv = conv_sum.astype(jnp.bfloat16).reshape(TOK_DEV, SHARD_HEADS, HEAD_DIM)
        cum = jnp.cumsum(decay_blk, axis=0)
        total = cum[-1]
        cum_heads = cum.T
        scores = jnp.einsum('thd,shd->hts', query_blk.astype(jnp.float32), key_conv.astype(jnp.float32))
        spread = cum_heads[:, :, None] - cum_heads[:, None, :]
        weights = jnp.where(causal[None], scores * jnp.exp(jnp.where(causal[None], spread, 0.0)), 0.0).astype(jnp.bfloat16)
        intra = jnp.einsum('hts,shd->thd', weights.astype(jnp.float32), value_blk.astype(jnp.float32))
        weighted_keys = (key_conv.astype(jnp.float32) * jnp.exp(total[None, :] - cum)[:, :, None]).astype(jnp.bfloat16)
        block_state = jnp.einsum('shd,she->hde', weighted_keys.astype(jnp.float32), value_blk.astype(jnp.float32))
        prefix_low = prefix.astype(jnp.bfloat16)
        inter = jnp.einsum('thd,hde->the', query_blk.astype(jnp.float32), prefix_low.astype(jnp.float32)) * jnp.exp(cum)[:, :, None]
        mixed = intra + inter
        scale_inv = lax.rsqrt(lax.optimization_barrier(jnp.mean(mixed * mixed, axis=2, keepdims=True)) + 1e-05)
        result = (mixed * scale_inv * gain_heads[None]).astype(jnp.bfloat16)
        new_prefix = jnp.exp(total)[:, None, None] * prefix + block_state
        return ((new_prefix, key_raw[TOK_DEV - (taps - 1):]), result.reshape(TOK_DEV, WIDTH))
    start_prefix = jnp.zeros((SHARD_HEADS, HEAD_DIM, HEAD_DIM), jnp.float32)
    start_tail = jnp.zeros((KERNEL - 1, WIDTH), jnp.bfloat16)
    carry_end, outputs = lax.scan(one_block, (start_prefix, start_tail), (query_blocks, key_blocks, value_blocks, decay_blocks))
    return outputs.reshape(SEQUENCE_TOKENS, WIDTH)
```

```python
import functools

import jax
import jax.numpy as jnp
from jax import lax
from jax.experimental import pallas as pl
from jax.experimental.pallas import tpu as pltpu
from jax.sharding import PartitionSpec as P

MESH = pl.DeviceIdType.MESH
F32 = jnp.float32
BF16 = jnp.bfloat16
PLANE = 4
GROUP = 4
TAIL = 16


def dot(a, b, contract, precision=None):
    return lax.dot_general(
        a, b, (contract, ((), ())), preferred_element_type=F32, precision=precision
    )


def kernel(
    n, q_hbm, k_hbm, v_hbm, ld_ref, w_ref, g_ref, out_hbm,
    q_s, k_s, v_s, out_s, halo, kx, kc_s, intra_s, cum_c, cum_t, dec, coef,
    s_all, s_low, x_recv, s_chip, y_send, y_recv, z_send, z_recv, b_send, pre,
    in_sem, halo_sem, dec_send_sem, dec_recv_sem, x_sem, y_sem, z_sem, b_sem, out_sem,
):
    rows, width = q_s.shape
    heads = ld_ref.shape[1]
    size = width // heads
    chunks = heads // GROUP
    taps = w_ref.shape[0]
    cols = GROUP * size
    planes = n // PLANE

    me = lax.axis_index("ctx")
    r = lax.rem(me, PLANE)
    z = lax.div(me, PLANE)
    core = lax.rem(me, 2)
    y = lax.div(r, 2)
    sibling = me + 1 - 2 * core
    across = me + 2 - 4 * y
    has_before = z > 0
    has_after = z < planes - 1

    k_in = pltpu.make_async_copy(k_hbm, k_s, in_sem.at[0])
    v_in = pltpu.make_async_copy(v_hbm, v_s, in_sem.at[1])
    q_in = pltpu.make_async_copy(q_hbm, q_s, in_sem.at[2])
    k_in.start()
    v_in.start()
    q_in.start()

    barrier = pltpu.get_barrier_semaphore()

    def greet(target):
        pl.semaphore_signal(barrier, inc=1, device_id={"ctx": target}, device_id_type=MESH)

    for off in range(1, PLANE):
        greet(z * PLANE + lax.rem(r + off, PLANE))
    links = (
        (has_before, me - PLANE),
        (has_after, me + PLANE),
        (jnp.logical_and(has_before, r == 0), me - 1),
        (jnp.logical_and(has_after, r == PLANE - 1), me + 1),
    )
    for there, target in links:
        @pl.when(there)
        def _(target=target):
            greet(target)

    t_at = lax.broadcasted_iota(jnp.int32, (rows, rows), 0)
    s_at = lax.broadcasted_iota(jnp.int32, (rows, rows), 1)
    lower = jnp.where(s_at <= t_at, 1.0, 0.0).astype(F32)
    upper = jnp.where(t_at <= s_at, 1.0, 0.0).astype(F32)
    log_decay = ld_ref[...]
    cum = dot(lower, log_decay, ((1,), (0,)), lax.Precision.HIGHEST)
    for c in range(chunks):
        cum_c[c, :, 0:GROUP] = cum[:, c * GROUP : (c + 1) * GROUP]
    cum_rows = dot(log_decay, upper, ((0,), (0,)), lax.Precision.HIGHEST)
    cum_t[...] = cum_rows
    dec[r] = jnp.broadcast_to(jnp.exp(cum_rows[:, rows - 1 : rows]), (heads, size))

    guests = PLANE - 1
    for there, _ in links:
        guests = guests + jnp.where(there, 1, 0)
    pl.semaphore_wait(barrier, guests)

    def halo_copy(target):
        return pltpu.make_async_remote_copy(
            src_ref=k_hbm.at[pl.ds(rows - TAIL, TAIL), :],
            dst_ref=halo,
            send_sem=halo_sem.at[0],
            recv_sem=halo_sem.at[1],
            device_id={"ctx": target},
            device_id_type=MESH,
        )

    @pl.when(me < n - 1)
    def _():
        halo_copy(me + 1).start()

    def dec_copy(off, slot):
        return pltpu.make_async_remote_copy(
            src_ref=dec.at[slot],
            dst_ref=dec.at[slot],
            send_sem=dec_send_sem.at[off - 1],
            recv_sem=dec_recv_sem.at[off - 1],
            device_id={"ctx": z * PLANE + lax.rem(r + off, PLANE)},
            device_id_type=MESH,
        )

    for off in range(1, PLANE):
        dec_copy(off, r).start()

    def x_copy(j):
        return pltpu.make_async_remote_copy(
            src_ref=s_low.at[j, pl.ds(2 * (1 - core), 2)],
            dst_ref=x_recv.at[j],
            send_sem=x_sem.at[0, j],
            recv_sem=x_sem.at[1, j],
            device_id={"ctx": sibling},
            device_id_type=MESH,
        )

    def y_copy(j):
        return pltpu.make_async_remote_copy(
            src_ref=y_send.at[j],
            dst_ref=y_recv.at[j],
            send_sem=y_sem.at[0, j],
            recv_sem=y_sem.at[1, j],
            device_id={"ctx": across},
            device_id_type=MESH,
        )

    def z_copy(j):
        return pltpu.make_async_remote_copy(
            src_ref=z_send.at[j],
            dst_ref=z_recv.at[j],
            send_sem=z_sem.at[0, j],
            recv_sem=z_sem.at[1, j],
            device_id={"ctx": me + PLANE},
            device_id_type=MESH,
        )

    def b_copy(j, owner):
        return pltpu.make_async_remote_copy(
            src_ref=b_send.at[j],
            dst_ref=pre.at[j, pl.ds(2 * owner, 2)],
            send_sem=b_sem.at[0, j],
            recv_sem=b_sem.at[1, j],
            device_id={"ctx": sibling},
            device_id_type=MESH,
        )

    def out_copy(j):
        here = pl.ds(pl.multiple_of(j * cols, cols), cols)
        return pltpu.make_async_copy(out_s.at[:, here], out_hbm.at[:, here], out_sem.at[j])

    @pl.when(jnp.logical_not(has_before))
    def _():
        z_recv[...] = jnp.zeros_like(z_recv)

    k_in.wait()
    v_in.wait()

    @pl.when(me == 0)
    def _():
        halo[...] = jnp.zeros_like(halo)

    @pl.when(me > 0)
    def _():
        halo_copy(me).wait_recv()

    def head_columns(j, i):
        return pl.ds(pl.multiple_of(j * cols + i * size, size), size)

    def states(j):
        wide = pl.ds(pl.multiple_of(j * cols, cols), cols)
        kx[0:8, :] = halo[:, wide].astype(F32)[TAIL - 8 : TAIL]
        kx[pl.ds(8, rows), :] = k_s[:, wide].astype(F32)
        cum_j = cum_c[j][:, 0:GROUP]
        fade = jnp.exp(cum_j[rows - 1 : rows, :] - cum_j)
        for i in range(GROUP):
            at = head_columns(j, i)
            near = slice(i * size, (i + 1) * size)
            total = w_ref[0:1, at] * kx[pl.ds(8, rows), near]
            for tap in range(1, taps):
                total = total + w_ref[tap : tap + 1, at] * kx[pl.ds(8 - tap, rows), near]
            conv = total.astype(BF16)
            kc_s[:, at] = conv
            weighted = (conv.astype(F32) * fade[:, i : i + 1]).astype(BF16)
            state = dot(weighted, v_s[:, at], ((0,), (0,)))
            s_all[j, i] = state
            s_low[j, i] = state.astype(BF16)

    def ordered(flag, mine, other):
        return jnp.where(flag, mine, other), jnp.where(flag, other, mine)

    def chip_states(j):
        for a in range(2):
            h = j * GROUP + 2 * core + a
            first, second = ordered(core == 0, s_all[j, 2 * core + a], x_recv[j, a].astype(F32))
            joined = dec[2 * y + 1, pl.ds(h, 1), :] * first + second
            s_chip[j, a] = joined
            y_send[j, a] = joined.astype(BF16)

    def state_step(j, carry):
        @pl.when(j < chunks)
        def _():
            states(j)
            x_copy(j).start()

        @pl.when(j == 0)
        def _():
            for off in range(1, PLANE):
                dec_copy(off, lax.rem(r - off + PLANE, PLANE)).wait_recv()
            coef[0] = dec[0] * dec[1]
            coef[1] = dec[2] * dec[3]
            coef[2] = dec[0] * dec[1] * (dec[2] * dec[3])

        @pl.when(j > 0)
        def _():
            x_copy(j - 1).wait_recv()
            chip_states(j - 1)
            y_copy(j - 1).start()

        return carry

    lax.fori_loop(0, chunks + 1, state_step, 0)
    q_in.wait()

    def within(j):
        cum_j = cum_c[j][:, 0:GROUP]
        for i in range(GROUP):
            at = head_columns(j, i)
            scores = dot(q_s[:, at], kc_s[:, at], ((1,), (1,)))
            spread = cum_j[:, i : i + 1] - cum_t[pl.ds(j * GROUP + i, 1), :]
            ratio = jnp.exp(jnp.where(s_at <= t_at, spread, -1e30))
            weights = (scores * ratio).astype(BF16)
            intra_s[:, at] = dot(weights, v_s[:, at], ((1,), (0,)))

    def prefixes(j):
        for a in range(2):
            h = pl.ds(j * GROUP + 2 * core + a, 1)
            first, second = ordered(y == 0, s_chip[j, a], y_recv[j, a].astype(F32))
            before = z_recv[j, a].astype(F32)
            plane = coef[1, h, :] * first + second
            z_send[j, a] = (coef[2, h, :] * before + plane).astype(BF16)
            base = jnp.where(y == 0, before, coef[0, h, :] * before + first)
            chip_first = jnp.where(core == 0, s_all[j, 2 * core + a], x_recv[j, a].astype(F32))
            next_base = dec[2 * y, h, :] * base + chip_first
            mine, other = ordered(core == 0, base, next_base)
            pre[j, 2 * core + a] = mine.astype(BF16)
            b_send[j, a] = other.astype(BF16)

    def finish(j):
        grow = jnp.exp(cum_c[j][:, 0:GROUP])
        for i in range(GROUP):
            at = head_columns(j, i)
            inter = dot(q_s[:, at], pre[j, i], ((1,), (0,)))
            mixed = intra_s[:, at] + inter * grow[:, i : i + 1]
            mean = jnp.mean(mixed * mixed, axis=1, keepdims=True)
            out_s[:, at] = (mixed * lax.rsqrt(mean + 1e-05) * g_ref[:, at]).astype(BF16)

    def prefix_step(j, carry):
        @pl.when(j < chunks)
        def _():
            within(j)
            y_copy(j).wait_recv()

            @pl.when(has_before)
            def _():
                z_copy(j).wait_recv()

            prefixes(j)

            @pl.when(has_after)
            def _():
                z_copy(j).start()

            b_copy(j, core).start()

        @pl.when(j > 0)
        def _():
            b_copy(j - 1, 1 - core).wait_recv()
            finish(j - 1)
            out_copy(j - 1).start()

        return carry

    lax.fori_loop(0, chunks + 1, prefix_step, 0)

    def drain(j, carry):
        x_copy(j).wait_send()
        y_copy(j).wait_send()
        b_copy(j, core).wait_send()

        @pl.when(has_after)
        def _():
            z_copy(j).wait_send()

        out_copy(j).wait()
        return carry

    lax.fori_loop(0, chunks, drain, 0)
    for off in range(1, PLANE):
        dec_copy(off, r).wait_send()

    @pl.when(me < n - 1)
    def _():
        halo_copy(me + 1).wait_send()


def on_device(n, queries, key_input, value_input, log_decay, conv_weight, norm_gain):
    rows, width = queries.shape
    heads = log_decay.shape[1]
    size = width // heads
    chunks = heads // GROUP
    pair = pltpu.VMEM((chunks, 2, size, size), BF16)
    pair_wide = pltpu.VMEM((chunks, 2, size, size), F32)
    hbm = pl.BlockSpec(memory_space=pl.ANY)
    vmem = pl.BlockSpec(memory_space=pltpu.VMEM)
    dma = pltpu.SemaphoreType.DMA
    block = pltpu.VMEM((rows, width), BF16)
    return pl.pallas_call(
        functools.partial(kernel, n),
        out_shape=jax.ShapeDtypeStruct((rows, width), BF16),
        in_specs=[hbm, hbm, hbm, vmem, vmem, vmem],
        out_specs=hbm,
        scratch_shapes=[
            block, block, block, block,
            pltpu.VMEM((TAIL, width), BF16),
            pltpu.VMEM((rows + 8, GROUP * size), F32),
            block,
            pltpu.VMEM((rows, width), F32),
            pltpu.VMEM((chunks, rows, size), F32),
            pltpu.VMEM((heads, rows), F32),
            pltpu.VMEM((PLANE, heads, size), F32),
            pltpu.VMEM((3, heads, size), F32),
            pltpu.VMEM((chunks, GROUP, size, size), F32),
            pltpu.VMEM((chunks, GROUP, size, size), BF16),
            pair, pair_wide, pair, pair, pair, pair, pair,
            pltpu.VMEM((chunks, GROUP, size, size), BF16),
            dma((3,)), dma((2,)), dma((PLANE - 1,)), dma((PLANE - 1,)),
            dma((2, chunks)), dma((2, chunks)), dma((2, chunks)), dma((2, chunks)),
            dma((chunks,)),
        ],
        compiler_params=pltpu.CompilerParams(
            collective_id=0, has_side_effects=True, vmem_limit_bytes=40 * 1024 * 1024
        ),
        name="decayed_attention",
    )(queries, key_input, value_input, log_decay, conv_weight, norm_gain.reshape(1, width))


def solution(mesh):
    rows = P(("groups", "ctx"), None)
    return jax.shard_map(
        functools.partial(on_device, mesh.shape["ctx"]),
        mesh=mesh,
        in_specs=(rows, rows, rows, rows, P(), P()),
        out_specs=rows,
        check_vma=False,
    )
```

```python
import functools

import jax
import jax.numpy as jnp
from jax import lax
from jax.experimental import pallas as pl
from jax.experimental.pallas import tpu as pltpu
from jax.sharding import PartitionSpec as P

MESH = pl.DeviceIdType.MESH
F32 = jnp.float32
BF16 = jnp.bfloat16
PLANE = 4
GROUP = 4
TAIL = 16


def dot(a, b, contract, precision=None):
    return lax.dot_general(
        a, b, (contract, ((), ())), preferred_element_type=F32, precision=precision
    )


def kernel(
    n, q_hbm, k_hbm, v_hbm, ld_ref, w_ref, g_ref, out_hbm,
    q_s, k_s, v_s, out_s, halo, kx, kc_s, intra_s, cum_c, cum_t, dec, coef,
    s_all, s_low, x_recv, s_chip, y_send, y_recv, z_send, z_recv, b_send, pre,
    in_sem, q_sem, halo_sem, dec_send_sem, dec_recv_sem, x_sem, y_sem, z_sem, b_sem, out_sem,
):
    rows, width = q_s.shape
    heads = ld_ref.shape[0]
    size = width // heads
    chunks = heads // GROUP
    taps = w_ref.shape[0]
    cols = GROUP * size
    planes = n // PLANE

    me = lax.axis_index("ctx")
    r = lax.rem(me, PLANE)
    z = lax.div(me, PLANE)
    core = lax.rem(me, 2)
    y = lax.div(r, 2)
    sibling = me + 1 - 2 * core
    across = me + 2 - 4 * y
    has_before = z > 0
    has_after = z < planes - 1

    def chunk_columns(j):
        return pl.ds(pl.multiple_of(j * cols, cols), cols)

    def load(source, target, kind, j):
        here = chunk_columns(j)
        return pltpu.make_async_copy(source.at[:, here], target.at[:, here], in_sem.at[kind, j])

    def start_loads(j, carry):
        load(k_hbm, k_s, 0, j).start()
        load(v_hbm, v_s, 1, j).start()
        return carry

    lax.fori_loop(0, chunks, start_loads, 0)
    q_in = pltpu.make_async_copy(q_hbm, q_s, q_sem)
    q_in.start()

    barrier = pltpu.get_barrier_semaphore()

    def greet(target):
        pl.semaphore_signal(barrier, inc=1, device_id={"ctx": target}, device_id_type=MESH)

    for off in range(1, PLANE):
        greet(z * PLANE + lax.rem(r + off, PLANE))
    links = (
        (has_before, me - PLANE),
        (has_after, me + PLANE),
        (jnp.logical_and(has_before, r == 0), me - 1),
        (jnp.logical_and(has_after, r == PLANE - 1), me + 1),
    )
    for there, target in links:
        @pl.when(there)
        def _(target=target):
            greet(target)

    t_at = lax.broadcasted_iota(jnp.int32, (rows, rows), 0)
    s_at = lax.broadcasted_iota(jnp.int32, (rows, rows), 1)
    lower = jnp.where(s_at <= t_at, 1.0, 0.0).astype(F32)
    upper = jnp.where(t_at <= s_at, 1.0, 0.0).astype(F32)
    log_decay = ld_ref[...]
    cum = dot(lower, log_decay, ((1,), (1,)), lax.Precision.HIGHEST)
    for c in range(chunks):
        cum_c[c, :, 0:GROUP] = cum[:, c * GROUP : (c + 1) * GROUP]
    cum_rows = dot(log_decay, upper, ((1,), (0,)), lax.Precision.HIGHEST)
    cum_t[...] = cum_rows
    dec[r] = jnp.broadcast_to(jnp.exp(cum_rows[:, rows - 1 : rows]), (heads, size))

    guests = PLANE - 1
    for there, _ in links:
        guests = guests + jnp.where(there, 1, 0)
    pl.semaphore_wait(barrier, guests)

    def halo_copy(target):
        return pltpu.make_async_remote_copy(
            src_ref=k_hbm.at[pl.ds(rows - TAIL, TAIL), :],
            dst_ref=halo,
            send_sem=halo_sem.at[0],
            recv_sem=halo_sem.at[1],
            device_id={"ctx": target},
            device_id_type=MESH,
        )

    @pl.when(me < n - 1)
    def _():
        halo_copy(me + 1).start()

    def dec_copy(off, slot):
        return pltpu.make_async_remote_copy(
            src_ref=dec.at[slot],
            dst_ref=dec.at[slot],
            send_sem=dec_send_sem.at[off - 1],
            recv_sem=dec_recv_sem.at[off - 1],
            device_id={"ctx": z * PLANE + lax.rem(r + off, PLANE)},
            device_id_type=MESH,
        )

    for off in range(1, PLANE):
        dec_copy(off, r).start()

    def x_copy(j):
        return pltpu.make_async_remote_copy(
            src_ref=s_low.at[j, pl.ds(2 * (1 - core), 2)],
            dst_ref=x_recv.at[j],
            send_sem=x_sem.at[0, j],
            recv_sem=x_sem.at[1, j],
            device_id={"ctx": sibling},
            device_id_type=MESH,
        )

    def y_copy(j):
        return pltpu.make_async_remote_copy(
            src_ref=y_send.at[j],
            dst_ref=y_recv.at[j],
            send_sem=y_sem.at[0, j],
            recv_sem=y_sem.at[1, j],
            device_id={"ctx": across},
            device_id_type=MESH,
        )

    def z_copy(j):
        return pltpu.make_async_remote_copy(
            src_ref=z_send.at[j],
            dst_ref=z_recv.at[j],
            send_sem=z_sem.at[0, j],
            recv_sem=z_sem.at[1, j],
            device_id={"ctx": me + PLANE},
            device_id_type=MESH,
        )

    def b_copy(j, owner):
        return pltpu.make_async_remote_copy(
            src_ref=b_send.at[j],
            dst_ref=pre.at[j, pl.ds(2 * owner, 2)],
            send_sem=b_sem.at[0, j],
            recv_sem=b_sem.at[1, j],
            device_id={"ctx": sibling},
            device_id_type=MESH,
        )

    def out_copy(j):
        here = chunk_columns(j)
        return pltpu.make_async_copy(out_s.at[:, here], out_hbm.at[:, here], out_sem.at[j])

    @pl.when(jnp.logical_not(has_before))
    def _():
        z_recv[...] = jnp.zeros_like(z_recv)

    @pl.when(me == 0)
    def _():
        halo[...] = jnp.zeros_like(halo)

    @pl.when(me > 0)
    def _():
        halo_copy(me).wait_recv()

    def head_columns(j, i):
        return pl.ds(pl.multiple_of(j * cols + i * size, size), size)

    def states(j):
        load(k_hbm, k_s, 0, j).wait()
        load(v_hbm, v_s, 1, j).wait()
        wide = chunk_columns(j)
        kx[0:8, :] = halo[:, wide].astype(F32)[TAIL - 8 : TAIL]
        kx[pl.ds(8, rows), :] = k_s[:, wide].astype(F32)
        cum_j = cum_c[j][:, 0:GROUP]
        fade = jnp.exp(cum_j[rows - 1 : rows, :] - cum_j)
        for i in range(GROUP):
            at = head_columns(j, i)
            near = slice(i * size, (i + 1) * size)
            total = w_ref[0:1, at] * kx[pl.ds(8, rows), near]
            for tap in range(1, taps):
                total = total + w_ref[tap : tap + 1, at] * kx[pl.ds(8 - tap, rows), near]
            conv = total.astype(BF16)
            kc_s[:, at] = conv
            weighted = (conv.astype(F32) * fade[:, i : i + 1]).astype(BF16)
            state = dot(weighted, v_s[:, at], ((0,), (0,)))
            s_all[j, i] = state
            s_low[j, i] = state.astype(BF16)

    def ordered(flag, mine, other):
        return jnp.where(flag, mine, other), jnp.where(flag, other, mine)

    def chip_states(j):
        for a in range(2):
            h = j * GROUP + 2 * core + a
            first, second = ordered(core == 0, s_all[j, 2 * core + a], x_recv[j, a].astype(F32))
            joined = dec[2 * y + 1, pl.ds(h, 1), :] * first + second
            s_chip[j, a] = joined
            y_send[j, a] = joined.astype(BF16)

    def within(j):
        cum_j = cum_c[j][:, 0:GROUP]
        for i in range(GROUP):
            at = head_columns(j, i)
            scores = dot(q_s[:, at], kc_s[:, at], ((1,), (1,)))
            spread = cum_j[:, i : i + 1] - cum_t[pl.ds(j * GROUP + i, 1), :]
            ratio = jnp.exp(jnp.where(s_at <= t_at, spread, -1e30))
            weights = (scores * ratio).astype(BF16)
            intra_s[:, at] = dot(weights, v_s[:, at], ((1,), (0,)))

    def prefixes(j):
        for a in range(2):
            h = pl.ds(j * GROUP + 2 * core + a, 1)
            first, second = ordered(y == 0, s_chip[j, a], y_recv[j, a].astype(F32))
            before = z_recv[j, a].astype(F32)
            plane = coef[1, h, :] * first + second
            z_send[j, a] = (coef[2, h, :] * before + plane).astype(BF16)
            base = jnp.where(y == 0, before, coef[0, h, :] * before + first)
            chip_first = jnp.where(core == 0, s_all[j, 2 * core + a], x_recv[j, a].astype(F32))
            next_base = dec[2 * y, h, :] * base + chip_first
            mine, other = ordered(core == 0, base, next_base)
            pre[j, 2 * core + a] = mine.astype(BF16)
            b_send[j, a] = other.astype(BF16)

    def finish(j):
        grow = jnp.exp(cum_c[j][:, 0:GROUP])
        for i in range(GROUP):
            at = head_columns(j, i)
            inter = dot(q_s[:, at], pre[j, i], ((1,), (0,)))
            mixed = intra_s[:, at] + inter * grow[:, i : i + 1]
            mean = jnp.mean(mixed * mixed, axis=1, keepdims=True)
            out_s[:, at] = (mixed * lax.rsqrt(mean + 1e-05) * g_ref[:, at]).astype(BF16)

    chain_lag = jnp.minimum(2 + 3 * z, chunks + 3)
    within_lag = chunks
    finish_lag = jnp.maximum(chain_lag + 2, within_lag + 1)

    def during(step, lag, work):
        j = step - lag

        @pl.when(jnp.logical_and(j >= 0, j < chunks))
        def _():
            work(j)

    def state_part(j):
        states(j)
        x_copy(j).start()

    def chip_part(j):
        x_copy(j).wait_recv()
        chip_states(j)
        y_copy(j).start()

    def chain_part(j):
        y_copy(j).wait_recv()

        @pl.when(has_before)
        def _():
            z_copy(j).wait_recv()

        prefixes(j)

        @pl.when(has_after)
        def _():
            z_copy(j).start()

        b_copy(j, core).start()

    def within_part(j):
        @pl.when(j == 0)
        def _():
            q_in.wait()

        within(j)

    def finish_part(j):
        b_copy(j, 1 - core).wait_recv()
        finish(j)
        out_copy(j).start()

    def one_step(step, carry):
        during(step, 0, state_part)

        @pl.when(step == 0)
        def _():
            for off in range(1, PLANE):
                dec_copy(off, lax.rem(r - off + PLANE, PLANE)).wait_recv()
            coef[0] = dec[0] * dec[1]
            coef[1] = dec[2] * dec[3]
            coef[2] = dec[0] * dec[1] * (dec[2] * dec[3])

        during(step, 1, chip_part)
        during(step, chain_lag, chain_part)
        during(step, within_lag, within_part)
        during(step, finish_lag, finish_part)
        return carry

    lax.fori_loop(0, 2 * chunks + 5, one_step, 0)

    def drain(j, carry):
        x_copy(j).wait_send()
        y_copy(j).wait_send()
        b_copy(j, core).wait_send()

        @pl.when(has_after)
        def _():
            z_copy(j).wait_send()

        out_copy(j).wait()
        return carry

    lax.fori_loop(0, chunks, drain, 0)
    for off in range(1, PLANE):
        dec_copy(off, r).wait_send()

    @pl.when(me < n - 1)
    def _():
        halo_copy(me + 1).wait_send()


def on_device(n, queries, key_input, value_input, log_decay, conv_weight, norm_gain):
    rows, width = queries.shape
    heads = log_decay.shape[1]
    size = width // heads
    chunks = heads // GROUP
    pair = pltpu.VMEM((chunks, 2, size, size), BF16)
    pair_wide = pltpu.VMEM((chunks, 2, size, size), F32)
    hbm = pl.BlockSpec(memory_space=pl.ANY)
    vmem = pl.BlockSpec(memory_space=pltpu.VMEM)
    dma = pltpu.SemaphoreType.DMA
    block = pltpu.VMEM((rows, width), BF16)
    return pl.pallas_call(
        functools.partial(kernel, n),
        out_shape=jax.ShapeDtypeStruct((rows, width), BF16),
        in_specs=[hbm, hbm, hbm, vmem, vmem, vmem],
        out_specs=hbm,
        scratch_shapes=[
            block, block, block, block,
            pltpu.VMEM((TAIL, width), BF16),
            pltpu.VMEM((rows + 8, GROUP * size), F32),
            block,
            pltpu.VMEM((rows, width), F32),
            pltpu.VMEM((chunks, rows, size), F32),
            pltpu.VMEM((heads, rows), F32),
            pltpu.VMEM((PLANE, heads, size), F32),
            pltpu.VMEM((3, heads, size), F32),
            pltpu.VMEM((chunks, GROUP, size, size), F32),
            pltpu.VMEM((chunks, GROUP, size, size), BF16),
            pair, pair_wide, pair, pair, pair, pair, pair,
            pltpu.VMEM((chunks, GROUP, size, size), BF16),
            dma((2, chunks)), dma, dma((2,)), dma((PLANE - 1,)), dma((PLANE - 1,)),
            dma((2, chunks)), dma((2, chunks)), dma((2, chunks)), dma((2, chunks)),
            dma((chunks,)),
        ],
        compiler_params=pltpu.CompilerParams(
            collective_id=0, has_side_effects=True, vmem_limit_bytes=60 * 1024 * 1024
        ),
        name="decayed_attention",
    )(queries, key_input, value_input, log_decay.T, conv_weight, norm_gain.reshape(1, width))


def solution(mesh):
    rows = P(("groups", "ctx"), None)
    return jax.shard_map(
        functools.partial(on_device, mesh.shape["ctx"]),
        mesh=mesh,
        in_specs=(rows, rows, rows, rows, P(), P()),
        out_specs=rows,
        check_vma=False,
    )
```

```python
import functools

import jax
import jax.numpy as jnp
from jax import lax
from jax.experimental import pallas as pl
from jax.experimental.pallas import tpu as pltpu
from jax.sharding import PartitionSpec as P

MESH = pl.DeviceIdType.MESH
F32 = jnp.float32
BF16 = jnp.bfloat16
PLANE = 4
GROUP = 4
TAIL = 16
PARTS = 4


def dot(a, b, contract, precision=None):
    return lax.dot_general(
        a, b, (contract, ((), ())), preferred_element_type=F32, precision=precision
    )


def kernel(
    n, q_hbm, k_hbm, v_hbm, ld_ref, w_ref, g_ref, out_hbm,
    q_s, k_s, v_s, out_s, tail, tail_out, tail_in, halo, kx, kc_s, intra_s, cum_c, cum_t, fade_t, dec, coef,
    s_all, s_low, x_recv, s_chip, y_send, y_recv, z_send, z_recv, b_send, pre,
    in_sem, q_sem, tail_sem, halo_sem, dec_send_sem, dec_recv_sem, x_sem, y_sem, z_sem, b_sem, out_sem,
):
    rows, width = q_s.shape
    heads = ld_ref.shape[0]
    size = width // heads
    chunks = heads // GROUP
    taps = w_ref.shape[0]
    cols = GROUP * size
    planes = n // PLANE

    me = lax.axis_index("ctx")
    r = lax.rem(me, PLANE)
    z = lax.div(me, PLANE)
    core = lax.rem(me, 2)
    y = lax.div(r, 2)
    sibling = me + 1 - 2 * core
    across = me + 2 - 4 * y
    has_before = z > 0
    has_after = z < planes - 1

    def chunk_columns(j):
        return pl.ds(pl.multiple_of(j * cols, cols), cols)

    def load(source, target, kind, j):
        here = chunk_columns(j)
        return pltpu.make_async_copy(source.at[:, here], target.at[:, here], in_sem.at[kind, j])

    tail_load = pltpu.make_async_copy(k_hbm.at[pl.ds(rows - TAIL, TAIL), :], tail, tail_sem)
    tail_load.start()

    def start_loads(j, carry):
        load(k_hbm, k_s, 0, j).start()
        load(v_hbm, v_s, 1, j).start()
        return carry

    lax.fori_loop(0, chunks, start_loads, 0)
    q_in = pltpu.make_async_copy(q_hbm, q_s, q_sem)
    q_in.start()

    barrier = pltpu.get_barrier_semaphore()

    def greet(target):
        pl.semaphore_signal(barrier, inc=1, device_id={"ctx": target}, device_id_type=MESH)

    for off in range(1, PLANE):
        greet(z * PLANE + lax.rem(r + off, PLANE))
    links = (
        (has_before, me - PLANE),
        (has_after, me + PLANE),
        (jnp.logical_and(has_before, r == 0), me - 1),
        (jnp.logical_and(has_after, r == PLANE - 1), me + 1),
    )
    for there, target in links:
        @pl.when(there)
        def _(target=target):
            greet(target)

    t_at = lax.broadcasted_iota(jnp.int32, (rows, rows), 0)
    s_at = lax.broadcasted_iota(jnp.int32, (rows, rows), 1)
    lower = jnp.where(s_at <= t_at, 1.0, 0.0).astype(F32)
    upper = jnp.where(t_at <= s_at, 1.0, 0.0).astype(F32)
    log_decay = ld_ref[...]
    cum = dot(lower, log_decay, ((1,), (1,)), lax.Precision.HIGHEST)
    for c in range(chunks):
        cum_c[c, :, 0:GROUP] = cum[:, c * GROUP : (c + 1) * GROUP]
    cum_rows = dot(log_decay, upper, ((1,), (0,)), lax.Precision.HIGHEST)
    cum_t[...] = cum_rows
    dec[r] = jnp.broadcast_to(jnp.exp(cum_rows[:, rows - 1 : rows]), (heads, size))

    fade_t[...] = jnp.exp(cum_rows[:, rows - 1 : rows] - cum_rows)
    keep = taps - 1
    part = width // PARTS
    tail_load.wait()
    last = tail[...].astype(F32)[TAIL - keep : TAIL]
    packed = [last[:, p * part : (p + 1) * part] for p in range(PARTS)]
    packed.append(jnp.zeros((TAIL - PARTS * keep, part), F32))
    tail_out[...] = jnp.concatenate(packed, axis=0).astype(BF16)

    guests = PLANE - 1
    for there, _ in links:
        guests = guests + jnp.where(there, 1, 0)
    pl.semaphore_wait(barrier, guests)

    def halo_copy(target):
        return pltpu.make_async_remote_copy(
            src_ref=tail_out,
            dst_ref=tail_in,
            send_sem=halo_sem.at[0],
            recv_sem=halo_sem.at[1],
            device_id={"ctx": target},
            device_id_type=MESH,
        )

    @pl.when(me < n - 1)
    def _():
        halo_copy(me + 1).start()

    def dec_copy(off, slot):
        return pltpu.make_async_remote_copy(
            src_ref=dec.at[slot],
            dst_ref=dec.at[slot],
            send_sem=dec_send_sem.at[off - 1],
            recv_sem=dec_recv_sem.at[off - 1],
            device_id={"ctx": z * PLANE + lax.rem(r + off, PLANE)},
            device_id_type=MESH,
        )

    for off in range(1, PLANE):
        dec_copy(off, r).start()

    def x_copy(j):
        return pltpu.make_async_remote_copy(
            src_ref=s_low.at[j, pl.ds(2 * (1 - core), 2)],
            dst_ref=x_recv.at[j],
            send_sem=x_sem.at[0, j],
            recv_sem=x_sem.at[1, j],
            device_id={"ctx": sibling},
            device_id_type=MESH,
        )

    def y_copy(j):
        return pltpu.make_async_remote_copy(
            src_ref=y_send.at[j],
            dst_ref=y_recv.at[j],
            send_sem=y_sem.at[0, j],
            recv_sem=y_sem.at[1, j],
            device_id={"ctx": across},
            device_id_type=MESH,
        )

    def z_copy(j):
        return pltpu.make_async_remote_copy(
            src_ref=z_send.at[j],
            dst_ref=z_recv.at[j],
            send_sem=z_sem.at[0, j],
            recv_sem=z_sem.at[1, j],
            device_id={"ctx": me + PLANE},
            device_id_type=MESH,
        )

    def b_copy(j, owner):
        return pltpu.make_async_remote_copy(
            src_ref=b_send.at[j],
            dst_ref=pre.at[j, pl.ds(2 * owner, 2)],
            send_sem=b_sem.at[0, j],
            recv_sem=b_sem.at[1, j],
            device_id={"ctx": sibling},
            device_id_type=MESH,
        )

    def out_copy(j):
        here = chunk_columns(j)
        return pltpu.make_async_copy(out_s.at[:, here], out_hbm.at[:, here], out_sem.at[j])

    @pl.when(jnp.logical_not(has_before))
    def _():
        z_recv[...] = jnp.zeros_like(z_recv)

    @pl.when(me == 0)
    def _():
        halo[...] = jnp.zeros_like(halo)

    @pl.when(me > 0)
    def _():
        halo_copy(me).wait_recv()
        got = tail_in[...].astype(F32)
        for p in range(PARTS):
            halo[8 - keep : 8, p * part : (p + 1) * part] = got[p * keep : (p + 1) * keep]

    def head_columns(j, i):
        return pl.ds(pl.multiple_of(j * cols + i * size, size), size)

    def states(j):
        load(k_hbm, k_s, 0, j).wait()
        load(v_hbm, v_s, 1, j).wait()
        wide = chunk_columns(j)
        kx[0:8, :] = halo[:, wide]
        kx[pl.ds(8, rows), :] = k_s[:, wide].astype(F32)
        taps_j = w_ref[:, wide]
        fade = [fade_t[pl.ds(j * GROUP + i, 1), :] for i in range(GROUP)]
        values = [v_s[:, head_columns(j, i)] for i in range(GROUP)]
        turned = []
        for i in range(GROUP):
            near = slice(i * size, (i + 1) * size)
            total = taps_j[0:1, near] * kx[pl.ds(8, rows), near]
            for tap in range(1, taps):
                total = total + taps_j[tap : tap + 1, near] * kx[pl.ds(8 - tap, rows), near]
            turned.append(total.T.astype(BF16))
        weighted = [(turned[i].astype(F32) * fade[i]).astype(BF16) for i in range(GROUP)]
        state = [dot(weighted[i], values[i], ((1,), (0,))) for i in range(GROUP)]
        for i in range(GROUP):
            kc_s[j, i] = turned[i]
            s_all[j, i] = state[i]
            s_low[j, i] = state[i].astype(BF16)

    def ordered(flag, mine, other):
        return jnp.where(flag, mine, other), jnp.where(flag, other, mine)

    def chip_states(j):
        for a in range(2):
            h = j * GROUP + 2 * core + a
            first, second = ordered(core == 0, s_all[j, 2 * core + a], x_recv[j, a].astype(F32))
            joined = dec[2 * y + 1, pl.ds(h, 1), :] * first + second
            s_chip[j, a] = joined
            y_send[j, a] = joined.astype(BF16)

    def within(j):
        cum_j = cum_c[j][:, 0:GROUP]
        each = range(GROUP)
        scores = [dot(q_s[:, head_columns(j, i)], kc_s[j, i], ((1,), (0,))) for i in each]
        values = [v_s[:, head_columns(j, i)] for i in each]
        ahead = [cum_t[pl.ds(j * GROUP + i, 1), :] for i in each]
        weights = []
        for i in each:
            spread = jnp.where(s_at <= t_at, cum_j[:, i : i + 1] - ahead[i], -1e30)
            weights.append((scores[i] * jnp.exp(spread)).astype(BF16))
        intra = [dot(weights[i], values[i], ((1,), (0,))) for i in each]
        for i in each:
            intra_s[:, head_columns(j, i)] = intra[i]

    def prefixes(j):
        for a in range(2):
            h = pl.ds(j * GROUP + 2 * core + a, 1)
            first, second = ordered(y == 0, s_chip[j, a], y_recv[j, a].astype(F32))
            before = z_recv[j, a].astype(F32)
            plane = coef[1, h, :] * first + second
            z_send[j, a] = (coef[2, h, :] * before + plane).astype(BF16)
            base = jnp.where(y == 0, before, coef[0, h, :] * before + first)
            chip_first = jnp.where(core == 0, s_all[j, 2 * core + a], x_recv[j, a].astype(F32))
            next_base = dec[2 * y, h, :] * base + chip_first
            mine, other = ordered(core == 0, base, next_base)
            pre[j, 2 * core + a] = mine.astype(BF16)
            b_send[j, a] = other.astype(BF16)

    def finish(j):
        grow = jnp.exp(cum_c[j][:, 0:GROUP])
        gain = g_ref[:, chunk_columns(j)]
        each = range(GROUP)
        inter = [dot(q_s[:, head_columns(j, i)], pre[j, i], ((1,), (0,))) for i in each]
        intra = [intra_s[:, head_columns(j, i)] for i in each]
        mixed = [intra[i] + inter[i] * grow[:, i : i + 1] for i in each]
        scale = [
            lax.rsqrt(jnp.mean(mixed[i] * mixed[i], axis=1, keepdims=True) + 1e-05) for i in each
        ]
        result = [
            (mixed[i] * scale[i] * gain[:, i * size : (i + 1) * size]).astype(BF16) for i in each
        ]
        for i in each:
            out_s[:, head_columns(j, i)] = result[i]

    chain_lag = jnp.minimum(4 + 3 * z, chunks + 4)
    within_lag = jnp.where(z < 2, chunks, chunks // 2)
    finish_lag = jnp.maximum(chain_lag + 2, within_lag + 1)

    def during(step, lag, work):
        j = step - lag

        @pl.when(jnp.logical_and(j >= 0, j < chunks))
        def _():
            work(j)

    def state_part(j):
        states(j)
        x_copy(j).start()

    def chip_part(j):
        x_copy(j).wait_recv()
        chip_states(j)
        y_copy(j).start()

    def chain_part(j):
        y_copy(j).wait_recv()

        @pl.when(has_before)
        def _():
            z_copy(j).wait_recv()

        prefixes(j)

        @pl.when(has_after)
        def _():
            z_copy(j).start()

        b_copy(j, core).start()

    def within_part(j):
        @pl.when(j == 0)
        def _():
            q_in.wait()

        within(j)

    def finish_part(j):
        b_copy(j, 1 - core).wait_recv()
        finish(j)
        out_copy(j).start()

    def one_step(step, carry):
        during(step, 0, state_part)

        @pl.when(step == 0)
        def _():
            for off in range(1, PLANE):
                dec_copy(off, lax.rem(r - off + PLANE, PLANE)).wait_recv()
            coef[0] = dec[0] * dec[1]
            coef[1] = dec[2] * dec[3]
            coef[2] = dec[0] * dec[1] * (dec[2] * dec[3])

        during(step, 1, chip_part)
        during(step, chain_lag, chain_part)
        during(step, within_lag, within_part)
        during(step, finish_lag, finish_part)
        return carry

    lax.fori_loop(0, 2 * chunks + 6, one_step, 0)

    def drain(j, carry):
        x_copy(j).wait_send()
        y_copy(j).wait_send()
        b_copy(j, core).wait_send()

        @pl.when(has_after)
        def _():
            z_copy(j).wait_send()

        out_copy(j).wait()
        return carry

    lax.fori_loop(0, chunks, drain, 0)
    for off in range(1, PLANE):
        dec_copy(off, r).wait_send()

    @pl.when(me < n - 1)
    def _():
        halo_copy(me + 1).wait_send()


def on_device(n, queries, key_input, value_input, log_decay, conv_weight, norm_gain):
    rows, width = queries.shape
    heads = log_decay.shape[1]
    size = width // heads
    chunks = heads // GROUP
    pair = pltpu.VMEM((chunks, 2, size, size), BF16)
    pair_wide = pltpu.VMEM((chunks, 2, size, size), F32)
    hbm = pl.BlockSpec(memory_space=pltpu.HBM)
    vmem = pl.BlockSpec(memory_space=pltpu.VMEM)
    dma = pltpu.SemaphoreType.DMA
    block = pltpu.VMEM((rows, width), BF16)
    return pl.pallas_call(
        functools.partial(kernel, n),
        out_shape=jax.ShapeDtypeStruct((rows, width), BF16),
        in_specs=[hbm, hbm, hbm, vmem, vmem, vmem],
        out_specs=pl.BlockSpec(memory_space=pl.ANY),
        scratch_shapes=[
            block, block, block, block,
            pltpu.VMEM((TAIL, width), BF16),
            pltpu.VMEM((TAIL, width // PARTS), BF16),
            pltpu.VMEM((TAIL, width // PARTS), BF16),
            pltpu.VMEM((8, width), F32),
            pltpu.VMEM((rows + 8, GROUP * size), F32),
            pltpu.VMEM((chunks, GROUP, size, rows), BF16),
            pltpu.VMEM((rows, width), F32),
            pltpu.VMEM((chunks, rows, size), F32),
            pltpu.VMEM((heads, rows), F32),
            pltpu.VMEM((heads, rows), F32),
            pltpu.VMEM((PLANE, heads, size), F32),
            pltpu.VMEM((3, heads, size), F32),
            pltpu.VMEM((chunks, GROUP, size, size), F32),
            pltpu.VMEM((chunks, GROUP, size, size), BF16),
            pair, pair_wide, pair, pair, pair, pair, pair,
            pltpu.VMEM((chunks, GROUP, size, size), BF16),
            dma((2, chunks)), dma, dma, dma((2,)), dma((PLANE - 1,)), dma((PLANE - 1,)),
            dma((2, chunks)), dma((2, chunks)), dma((2, chunks)), dma((2, chunks)),
            dma((chunks,)),
        ],
        compiler_params=pltpu.CompilerParams(
            collective_id=0, has_side_effects=True, vmem_limit_bytes=52 * 1024 * 1024
        ),
        name="decayed_attention",
    )(queries, key_input, value_input, log_decay.T, conv_weight, norm_gain.reshape(1, width))


def solution(mesh):
    rows = P(("groups", "ctx"), None)
    return jax.shard_map(
        functools.partial(on_device, mesh.shape["ctx"]),
        mesh=mesh,
        in_specs=(rows, rows, rows, rows, P(), P()),
        out_specs=rows,
        check_vma=False,
    )
```

```python
import functools

import jax
import jax.numpy as jnp
from jax import lax
from jax.experimental import pallas as pl
from jax.experimental.pallas import tpu as pltpu
from jax.sharding import PartitionSpec as P

MESH = pl.DeviceIdType.MESH
F32 = jnp.float32
BF16 = jnp.bfloat16
PLANE = 4
GROUP = 4
TAIL = 16
PARTS = 4


def dot(a, b, contract, precision=None):
    return lax.dot_general(
        a, b, (contract, ((), ())), preferred_element_type=F32, precision=precision
    )


def kernel(
    n, q_hbm, k_hbm, v_hbm, ld_hbm, w_hbm, g_hbm, out_hbm,
    ld_ref, w_ref, g_ref, q_s, k_s, v_s, out_s, tail, tail_out, tail_in, halo, kx, kc_s, intra_s, cum_c, cum_t, fade_t, dec, coef,
    s_all, s_low, x_recv, s_chip, y_send, y_recv, z_send, z_recv, r_send, base, b_send, pre,
    in_sem, q_sem, tail_sem, small_sem, halo_sem, dec_send_sem, dec_recv_sem, x_sem, y_sem, z_sem, r_sem, b_sem, out_sem,
):
    rows, width = q_s.shape
    heads = ld_ref.shape[0]
    size = width // heads
    chunks = heads // GROUP
    taps = w_ref.shape[0]
    cols = GROUP * size
    planes = n // PLANE

    me = lax.axis_index("ctx")
    r = lax.rem(me, PLANE)
    z = lax.div(me, PLANE)
    core = lax.rem(me, 2)
    y = lax.div(r, 2)
    sibling = me + 1 - 2 * core
    across = me + 2 - 4 * y
    has_before = z > 0
    has_after = z < planes - 1

    def chunk_columns(j):
        return pl.ds(pl.multiple_of(j * cols, cols), cols)

    def load(source, target, kind, j):
        here = chunk_columns(j)
        return pltpu.make_async_copy(source.at[:, here], target.at[:, here], in_sem.at[kind, j])

    small = [
        pltpu.make_async_copy(source, target, small_sem.at[at])
        for at, (source, target) in enumerate(((ld_hbm, ld_ref), (w_hbm, w_ref), (g_hbm, g_ref)))
    ]
    small[0].start()
    tail_load = pltpu.make_async_copy(k_hbm.at[pl.ds(rows - TAIL, TAIL), :], tail, tail_sem)
    tail_load.start()
    small[1].start()

    def start_loads(j, carry):
        load(k_hbm, k_s, 0, j).start()
        load(v_hbm, v_s, 1, j).start()
        return carry

    lax.fori_loop(0, chunks, start_loads, 0)
    q_in = pltpu.make_async_copy(q_hbm, q_s, q_sem)
    q_in.start()
    small[2].start()

    barrier = pltpu.get_barrier_semaphore()

    def greet(target):
        pl.semaphore_signal(barrier, inc=1, device_id={"ctx": target}, device_id_type=MESH)

    for off in range(1, PLANE):
        greet(z * PLANE + lax.rem(r + off, PLANE))
    links = (
        (has_before, me - PLANE),
        (has_after, me + PLANE),
        (jnp.logical_and(has_before, r == 0), me - 1),
        (jnp.logical_and(has_after, r == PLANE - 1), me + 1),
    )
    for there, target in links:
        @pl.when(there)
        def _(target=target):
            greet(target)

    t_at = lax.broadcasted_iota(jnp.int32, (rows, rows), 0)
    s_at = lax.broadcasted_iota(jnp.int32, (rows, rows), 1)
    lower = jnp.where(s_at <= t_at, 1.0, 0.0).astype(F32)
    upper = jnp.where(t_at <= s_at, 1.0, 0.0).astype(F32)
    small[0].wait()
    log_decay = ld_ref[...]
    cum = dot(lower, log_decay, ((1,), (1,)), lax.Precision.HIGHEST)
    for c in range(chunks):
        cum_c[c, :, 0:GROUP] = cum[:, c * GROUP : (c + 1) * GROUP]
    cum_rows = dot(log_decay, upper, ((1,), (0,)), lax.Precision.HIGHEST)
    cum_t[...] = cum_rows
    dec[r] = jnp.broadcast_to(jnp.exp(cum_rows[:, rows - 1 : rows]), (heads, size))

    fade_t[...] = jnp.exp(cum_rows[:, rows - 1 : rows] - cum_rows)
    keep = taps - 1
    part = width // PARTS
    tail_load.wait()
    last = tail[...].astype(F32)[TAIL - keep : TAIL]
    packed = [last[:, p * part : (p + 1) * part] for p in range(PARTS)]
    packed.append(jnp.zeros((TAIL - PARTS * keep, part), F32))
    tail_out[...] = jnp.concatenate(packed, axis=0).astype(BF16)

    guests = PLANE - 1
    for there, _ in links:
        guests = guests + jnp.where(there, 1, 0)
    pl.semaphore_wait(barrier, guests)

    def halo_copy(target):
        return pltpu.make_async_remote_copy(
            src_ref=tail_out,
            dst_ref=tail_in,
            send_sem=halo_sem.at[0],
            recv_sem=halo_sem.at[1],
            device_id={"ctx": target},
            device_id_type=MESH,
        )

    @pl.when(me < n - 1)
    def _():
        halo_copy(me + 1).start()

    def dec_copy(off, slot):
        return pltpu.make_async_remote_copy(
            src_ref=dec.at[slot],
            dst_ref=dec.at[slot],
            send_sem=dec_send_sem.at[off - 1],
            recv_sem=dec_recv_sem.at[off - 1],
            device_id={"ctx": z * PLANE + lax.rem(r + off, PLANE)},
            device_id_type=MESH,
        )

    for off in range(1, PLANE):
        dec_copy(off, r).start()

    def x_copy(j):
        return pltpu.make_async_remote_copy(
            src_ref=s_low.at[j, pl.ds(2 * (1 - core), 2)],
            dst_ref=x_recv.at[j],
            send_sem=x_sem.at[0, j],
            recv_sem=x_sem.at[1, j],
            device_id={"ctx": sibling},
            device_id_type=MESH,
        )

    def y_copy(j):
        return pltpu.make_async_remote_copy(
            src_ref=y_send.at[j],
            dst_ref=y_recv.at[j],
            send_sem=y_sem.at[0, j],
            recv_sem=y_sem.at[1, j],
            device_id={"ctx": across},
            device_id_type=MESH,
        )

    def z_copy(j):
        return pltpu.make_async_remote_copy(
            src_ref=z_send.at[j],
            dst_ref=z_recv.at[j],
            send_sem=z_sem.at[0, j],
            recv_sem=z_sem.at[1, j],
            device_id={"ctx": me + PLANE},
            device_id_type=MESH,
        )

    def r_copy(j, owner):
        return pltpu.make_async_remote_copy(
            src_ref=r_send.at[j],
            dst_ref=base.at[j, owner],
            send_sem=r_sem.at[0, j],
            recv_sem=r_sem.at[1, j],
            device_id={"ctx": across},
            device_id_type=MESH,
        )

    def b_copy(j, owner):
        return pltpu.make_async_remote_copy(
            src_ref=b_send.at[j],
            dst_ref=pre.at[j, pl.ds(2 * owner, 2)],
            send_sem=b_sem.at[0, j],
            recv_sem=b_sem.at[1, j],
            device_id={"ctx": sibling},
            device_id_type=MESH,
        )

    def out_copy(j):
        here = chunk_columns(j)
        return pltpu.make_async_copy(out_s.at[:, here], out_hbm.at[:, here], out_sem.at[j])

    @pl.when(jnp.logical_not(has_before))
    def _():
        z_recv[...] = jnp.zeros_like(z_recv)

    small[1].wait()

    @pl.when(me == 0)
    def _():
        halo[...] = jnp.zeros_like(halo)

    @pl.when(me > 0)
    def _():
        halo_copy(me).wait_recv()
        got = tail_in[...].astype(F32)
        for p in range(PARTS):
            halo[8 - keep : 8, p * part : (p + 1) * part] = got[p * keep : (p + 1) * keep]

    def head_columns(j, i):
        return pl.ds(pl.multiple_of(j * cols + i * size, size), size)

    def states(j):
        load(k_hbm, k_s, 0, j).wait()
        load(v_hbm, v_s, 1, j).wait()
        wide = chunk_columns(j)
        kx[0:8, :] = halo[:, wide]
        kx[pl.ds(8, rows), :] = k_s[:, wide].astype(F32)
        taps_j = w_ref[:, wide]
        fade = [fade_t[pl.ds(j * GROUP + i, 1), :] for i in range(GROUP)]
        values = [v_s[:, head_columns(j, i)] for i in range(GROUP)]
        turned = []
        for i in range(GROUP):
            near = slice(i * size, (i + 1) * size)
            total = taps_j[0:1, near] * kx[pl.ds(8, rows), near]
            for tap in range(1, taps):
                total = total + taps_j[tap : tap + 1, near] * kx[pl.ds(8 - tap, rows), near]
            turned.append(total.T.astype(BF16))
        weighted = [(turned[i].astype(F32) * fade[i]).astype(BF16) for i in range(GROUP)]
        state = [dot(weighted[i], values[i], ((1,), (0,))) for i in range(GROUP)]
        for i in range(GROUP):
            kc_s[j, i] = turned[i]
            s_all[j, i] = state[i]
            s_low[j, i] = state[i].astype(BF16)

    def ordered(flag, mine, other):
        return jnp.where(flag, mine, other), jnp.where(flag, other, mine)

    def chip_states(j):
        for a in range(2):
            h = j * GROUP + 2 * core + a
            first, second = ordered(core == 0, s_all[j, 2 * core + a], x_recv[j, a].astype(F32))
            joined = dec[2 * y + 1, pl.ds(h, 1), :] * first + second
            s_chip[j, a] = joined
        y_send[j] = s_chip[j, 1 - y].astype(BF16)

    def within(j):
        cum_j = cum_c[j][:, 0:GROUP]
        each = range(GROUP)
        scores = [dot(q_s[:, head_columns(j, i)], kc_s[j, i], ((1,), (0,))) for i in each]
        values = [v_s[:, head_columns(j, i)] for i in each]
        ahead = [cum_t[pl.ds(j * GROUP + i, 1), :] for i in each]
        weights = []
        for i in each:
            spread = jnp.where(s_at <= t_at, cum_j[:, i : i + 1] - ahead[i], -1e30)
            weights.append((scores[i] * jnp.exp(spread)).astype(BF16))
        intra = [dot(weights[i], values[i], ((1,), (0,))) for i in each]
        for i in each:
            intra_s[:, head_columns(j, i)] = intra[i]

    def advance(j):
        h = pl.ds(j * GROUP + 2 * core + y, 1)
        first, second = ordered(y == 0, s_chip[j, y], y_recv[j].astype(F32))
        before = z_recv[j].astype(F32)
        plane = coef[1, h, :] * first + second
        z_send[j] = (coef[2, h, :] * before + plane).astype(BF16)
        mine, other = ordered(y == 0, before, coef[0, h, :] * before + first)
        r_send[j] = other.astype(BF16)
        base[j, y] = mine.astype(BF16)

    def prefixes(j):
        for a in range(2):
            h = pl.ds(j * GROUP + 2 * core + a, 1)
            chip_base = base[j, a].astype(F32)
            chip_first = jnp.where(core == 0, s_all[j, 2 * core + a], x_recv[j, a].astype(F32))
            next_base = dec[2 * y, h, :] * chip_base + chip_first
            mine, other = ordered(core == 0, chip_base, next_base)
            pre[j, 2 * core + a] = mine.astype(BF16)
            b_send[j, a] = other.astype(BF16)

    def finish(j):
        grow = jnp.exp(cum_c[j][:, 0:GROUP])
        gain = g_ref[:, chunk_columns(j)]
        each = range(GROUP)
        inter = [dot(q_s[:, head_columns(j, i)], pre[j, i], ((1,), (0,))) for i in each]
        intra = [intra_s[:, head_columns(j, i)] for i in each]
        mixed = [intra[i] + inter[i] * grow[:, i : i + 1] for i in each]
        scale = [
            lax.rsqrt(jnp.mean(mixed[i] * mixed[i], axis=1, keepdims=True) + 1e-05) for i in each
        ]
        result = [
            (mixed[i] * scale[i] * gain[:, i * size : (i + 1) * size]).astype(BF16) for i in each
        ]
        for i in each:
            out_s[:, head_columns(j, i)] = result[i]

    chain_lag = jnp.minimum(4 + lax.div(5 * z, 2), chunks + 3)
    within_lag = jnp.where(z < 2, chunks, chunks // 2)
    prefix_lag = chain_lag + 3
    finish_lag = jnp.maximum(prefix_lag + 2, within_lag + 1)

    def during(step, lag, work):
        j = step - lag

        @pl.when(jnp.logical_and(j >= 0, j < chunks))
        def _():
            work(j)

    def state_part(j):
        states(j)
        x_copy(j).start()

    def chip_part(j):
        x_copy(j).wait_recv()
        chip_states(j)
        y_copy(j).start()

    def chain_part(j):
        y_copy(j).wait_recv()

        @pl.when(has_before)
        def _():
            z_copy(j).wait_recv()

        advance(j)

        @pl.when(has_after)
        def _():
            z_copy(j).start()

        r_copy(j, y).start()

    def prefix_part(j):
        r_copy(j, 1 - y).wait_recv()
        prefixes(j)
        b_copy(j, core).start()

    def within_part(j):
        @pl.when(j == 0)
        def _():
            q_in.wait()
            small[2].wait()

        within(j)

    def finish_part(j):
        b_copy(j, 1 - core).wait_recv()
        finish(j)
        out_copy(j).start()

    def one_step(step, carry):
        during(step, 0, state_part)

        @pl.when(step == 0)
        def _():
            for off in range(1, PLANE):
                dec_copy(off, lax.rem(r - off + PLANE, PLANE)).wait_recv()
            coef[0] = dec[0] * dec[1]
            coef[1] = dec[2] * dec[3]
            coef[2] = dec[0] * dec[1] * (dec[2] * dec[3])

        during(step, 1, chip_part)
        during(step, chain_lag, chain_part)
        during(step, prefix_lag, prefix_part)
        during(step, within_lag, within_part)
        during(step, finish_lag, finish_part)
        return carry

    lax.fori_loop(0, 2 * chunks + 8, one_step, 0)

    def drain(j, carry):
        x_copy(j).wait_send()
        y_copy(j).wait_send()
        r_copy(j, y).wait_send()
        b_copy(j, core).wait_send()

        @pl.when(has_after)
        def _():
            z_copy(j).wait_send()

        out_copy(j).wait()
        return carry

    lax.fori_loop(0, chunks, drain, 0)
    for off in range(1, PLANE):
        dec_copy(off, r).wait_send()

    @pl.when(me < n - 1)
    def _():
        halo_copy(me + 1).wait_send()


def on_device(n, queries, key_input, value_input, log_decay, conv_weight, norm_gain):
    rows, width = queries.shape
    heads = log_decay.shape[1]
    size = width // heads
    chunks = heads // GROUP
    pair = pltpu.VMEM((chunks, 2, size, size), BF16)
    one = pltpu.VMEM((chunks, size, size), BF16)
    pair_wide = pltpu.VMEM((chunks, 2, size, size), F32)
    hbm = pl.BlockSpec(memory_space=pltpu.HBM)
    dma = pltpu.SemaphoreType.DMA
    block = pltpu.VMEM((rows, width), BF16)
    arguments = (
        queries, key_input, value_input, log_decay.T, conv_weight, norm_gain.reshape(1, width)
    )
    return pl.pallas_call(
        functools.partial(kernel, n),
        out_shape=jax.ShapeDtypeStruct((rows, width), BF16),
        in_specs=[hbm] * 6,
        out_specs=pl.BlockSpec(memory_space=pl.ANY),
        scratch_shapes=[
            pltpu.VMEM((heads, rows), F32),
            pltpu.VMEM(conv_weight.shape, F32),
            pltpu.VMEM((1, width), F32),
            block, block, block, block,
            pltpu.VMEM((TAIL, width), BF16),
            pltpu.VMEM((TAIL, width // PARTS), BF16),
            pltpu.VMEM((TAIL, width // PARTS), BF16),
            pltpu.VMEM((8, width), F32),
            pltpu.VMEM((rows + 8, GROUP * size), F32),
            pltpu.VMEM((chunks, GROUP, size, rows), BF16),
            pltpu.VMEM((rows, width), F32),
            pltpu.VMEM((chunks, rows, size), F32),
            pltpu.VMEM((heads, rows), F32),
            pltpu.VMEM((heads, rows), F32),
            pltpu.VMEM((PLANE, heads, size), F32),
            pltpu.VMEM((3, heads, size), F32),
            pltpu.VMEM((chunks, GROUP, size, size), F32),
            pltpu.VMEM((chunks, GROUP, size, size), BF16),
            pair, pair_wide, one, one, one, one, one, pair, pair,
            pltpu.VMEM((chunks, GROUP, size, size), BF16),
            dma((2, chunks)), dma, dma, dma((3,)), dma((2,)), dma((PLANE - 1,)), dma((PLANE - 1,)),
            dma((2, chunks)), dma((2, chunks)), dma((2, chunks)), dma((2, chunks)), dma((2, chunks)),
            dma((chunks,)),
        ],
        compiler_params=pltpu.CompilerParams(
            collective_id=0, has_side_effects=True, vmem_limit_bytes=52 * 1024 * 1024
        ),
        name="decayed_attention",
    )(*(pltpu.with_memory_space_constraint(x, pltpu.HBM) for x in arguments))


def solution(mesh):
    rows = P(("groups", "ctx"), None)
    return jax.shard_map(
        functools.partial(on_device, mesh.shape["ctx"]),
        mesh=mesh,
        in_specs=(rows, rows, rows, rows, P(), P()),
        out_specs=rows,
        check_vma=False,
    )
```

```python
import functools

import jax
import jax.numpy as jnp
from jax import lax
from jax.experimental import pallas as pl
from jax.experimental.pallas import tpu as pltpu
from jax.sharding import PartitionSpec as P

MESH = pl.DeviceIdType.MESH
F32 = jnp.float32
BF16 = jnp.bfloat16
PLANE = 4
GROUP = 4
BATCH = 2
TAIL = 16
PARTS = 4


def dot(a, b, contract, precision=None):
    return lax.dot_general(
        a, b, (contract, ((), ())), preferred_element_type=F32, precision=precision
    )


def kernel(
    n, q_hbm, k_hbm, v_hbm, ld_hbm, w_hbm, g_hbm, out_hbm,
    ld_ref, w_ref, g_ref, q_s, k_s, v_s, out_s, tail, tail_out, tail_in, halo, kx, kc_s, intra_s, cum_c, cum_t, fade_t, dec, coef,
    s_all, s_low, x_recv, s_chip, y_send, y_recv, z_send, z_recv, r_send, base, b_send, pre,
    in_sem, q_sem, tail_sem, small_sem, halo_sem, dec_send_sem, dec_recv_sem, x_sem, y_sem, z_sem, r_sem, b_sem, out_sem,
):
    rows, width = q_s.shape
    heads = ld_ref.shape[0]
    size = width // heads
    chunks = heads // GROUP
    taps = w_ref.shape[0]
    cols = GROUP * size
    planes = n // PLANE

    me = lax.axis_index("ctx")
    r = lax.rem(me, PLANE)
    z = lax.div(me, PLANE)
    core = lax.rem(me, 2)
    y = lax.div(r, 2)
    sibling = me + 1 - 2 * core
    across = me + 2 - 4 * y
    has_before = z > 0
    has_after = z < planes - 1

    barrier = pltpu.get_barrier_semaphore()

    def greet(target):
        pl.semaphore_signal(barrier, inc=1, device_id={"ctx": target}, device_id_type=MESH)

    for off in range(1, PLANE):
        greet(z * PLANE + lax.rem(r + off, PLANE))
    links = (
        (has_before, me - PLANE),
        (has_after, me + PLANE),
        (jnp.logical_and(has_before, r == 0), me - 1),
        (jnp.logical_and(has_after, r == PLANE - 1), me + 1),
    )
    for there, target in links:
        @pl.when(there)
        def _(target=target):
            greet(target)

    batches = chunks // BATCH
    each = [(c, i) for c in range(BATCH) for i in range(GROUP)]

    def chunk_columns(j):
        return pl.ds(pl.multiple_of(j * cols, cols), cols)

    def batch_columns(b):
        return pl.ds(pl.multiple_of(b * BATCH * cols, BATCH * cols), BATCH * cols)

    def load(source, target, kind, j):
        here = batch_columns(j)
        return pltpu.make_async_copy(source.at[:, here], target.at[:, here], in_sem.at[kind, j])

    small = [
        pltpu.make_async_copy(source, target, small_sem.at[at])
        for at, (source, target) in enumerate(((ld_hbm, ld_ref), (w_hbm, w_ref), (g_hbm, g_ref)))
    ]
    small[0].start()
    tail_load = pltpu.make_async_copy(k_hbm.at[pl.ds(rows - TAIL, TAIL), :], tail, tail_sem)
    tail_load.start()
    small[1].start()

    def start_loads(j, carry):
        load(k_hbm, k_s, 0, j).start()
        load(v_hbm, v_s, 1, j).start()
        return carry

    lax.fori_loop(0, batches, start_loads, 0)
    q_in = pltpu.make_async_copy(q_hbm, q_s, q_sem)
    q_in.start()
    small[2].start()

    t_at = lax.broadcasted_iota(jnp.int32, (rows, rows), 0)
    s_at = lax.broadcasted_iota(jnp.int32, (rows, rows), 1)
    lower = jnp.where(s_at <= t_at, 1.0, 0.0).astype(F32)
    upper = jnp.where(t_at <= s_at, 1.0, 0.0).astype(F32)
    small[0].wait()
    log_decay = ld_ref[...]
    cum = dot(lower, log_decay, ((1,), (1,)), lax.Precision.HIGHEST)
    for c in range(chunks):
        cum_c[c, :, 0:GROUP] = cum[:, c * GROUP : (c + 1) * GROUP]
    cum_rows = dot(log_decay, upper, ((1,), (0,)), lax.Precision.HIGHEST)
    cum_t[...] = cum_rows
    dec[r] = jnp.broadcast_to(jnp.exp(cum_rows[:, rows - 1 : rows]), (heads, size))

    fade_t[...] = jnp.exp(cum_rows[:, rows - 1 : rows] - cum_rows)
    keep = taps - 1
    part = width // PARTS
    tail_load.wait()
    last = tail[...].astype(F32)[TAIL - keep : TAIL]
    packed = [last[:, p * part : (p + 1) * part] for p in range(PARTS)]
    packed.append(jnp.zeros((TAIL - PARTS * keep, part), F32))
    tail_out[...] = jnp.concatenate(packed, axis=0).astype(BF16)

    guests = PLANE - 1
    for there, _ in links:
        guests = guests + jnp.where(there, 1, 0)
    pl.semaphore_wait(barrier, guests)

    def halo_copy(target):
        return pltpu.make_async_remote_copy(
            src_ref=tail_out,
            dst_ref=tail_in,
            send_sem=halo_sem.at[0],
            recv_sem=halo_sem.at[1],
            device_id={"ctx": target},
            device_id_type=MESH,
        )

    @pl.when(me < n - 1)
    def _():
        halo_copy(me + 1).start()

    def dec_copy(off, slot):
        return pltpu.make_async_remote_copy(
            src_ref=dec.at[slot],
            dst_ref=dec.at[slot],
            send_sem=dec_send_sem.at[off - 1],
            recv_sem=dec_recv_sem.at[off - 1],
            device_id={"ctx": z * PLANE + lax.rem(r + off, PLANE)},
            device_id_type=MESH,
        )

    for off in range(1, PLANE):
        dec_copy(off, r).start()

    def x_copy(j):
        return pltpu.make_async_remote_copy(
            src_ref=s_low.at[j, pl.ds(2 * (1 - core), 2)],
            dst_ref=x_recv.at[j],
            send_sem=x_sem.at[0, j],
            recv_sem=x_sem.at[1, j],
            device_id={"ctx": sibling},
            device_id_type=MESH,
        )

    def y_copy(j):
        return pltpu.make_async_remote_copy(
            src_ref=y_send.at[j],
            dst_ref=y_recv.at[j],
            send_sem=y_sem.at[0, j],
            recv_sem=y_sem.at[1, j],
            device_id={"ctx": across},
            device_id_type=MESH,
        )

    def z_copy(j):
        return pltpu.make_async_remote_copy(
            src_ref=z_send.at[j],
            dst_ref=z_recv.at[j],
            send_sem=z_sem.at[0, j],
            recv_sem=z_sem.at[1, j],
            device_id={"ctx": me + PLANE},
            device_id_type=MESH,
        )

    def r_copy(j, owner):
        return pltpu.make_async_remote_copy(
            src_ref=r_send.at[j],
            dst_ref=base.at[j, owner],
            send_sem=r_sem.at[0, j],
            recv_sem=r_sem.at[1, j],
            device_id={"ctx": across},
            device_id_type=MESH,
        )

    def b_copy(j, owner):
        return pltpu.make_async_remote_copy(
            src_ref=b_send.at[j],
            dst_ref=pre.at[j, pl.ds(2 * owner, 2)],
            send_sem=b_sem.at[0, j],
            recv_sem=b_sem.at[1, j],
            device_id={"ctx": sibling},
            device_id_type=MESH,
        )

    def out_copy(j):
        here = chunk_columns(j)
        return pltpu.make_async_copy(out_s.at[:, here], out_hbm.at[:, here], out_sem.at[j])

    @pl.when(jnp.logical_not(has_before))
    def _():
        z_recv[...] = jnp.zeros_like(z_recv)

    small[1].wait()

    @pl.when(me == 0)
    def _():
        halo[...] = jnp.zeros_like(halo)

    @pl.when(me > 0)
    def _():
        halo_copy(me).wait_recv()
        got = tail_in[...].astype(F32)
        for p in range(PARTS):
            halo[8 - keep : 8, p * part : (p + 1) * part] = got[p * keep : (p + 1) * keep]

    def head_columns(j, i):
        return pl.ds(pl.multiple_of(j * cols + i * size, size), size)

    def states(b):
        load(k_hbm, k_s, 0, b).wait()
        load(v_hbm, v_s, 1, b).wait()
        wide = batch_columns(b)
        kx[0:8, :] = halo[:, wide]
        kx[pl.ds(8, rows), :] = k_s[:, wide].astype(F32)
        taps_b = w_ref[:, wide]
        fade = [fade_t[pl.ds((b * BATCH + c) * GROUP + i, 1), :] for c, i in each]
        values = [v_s[:, head_columns(b * BATCH + c, i)] for c, i in each]
        turned = []
        for c, i in each:
            near = slice((c * GROUP + i) * size, (c * GROUP + i + 1) * size)
            total = taps_b[0:1, near] * kx[pl.ds(8, rows), near]
            for tap in range(1, taps):
                total = total + taps_b[tap : tap + 1, near] * kx[pl.ds(8 - tap, rows), near]
            turned.append(total.astype(BF16).T)
        weighted = [(t.astype(F32) * f).astype(BF16) for t, f in zip(turned, fade)]
        state = [dot(w, v, ((1,), (0,))) for w, v in zip(weighted, values)]
        for at, (c, i) in enumerate(each):
            kc_s[b * BATCH + c, i] = turned[at]
            s_all[b * BATCH + c, i] = state[at]
            s_low[b * BATCH + c, i] = state[at].astype(BF16)

    def ordered(flag, mine, other):
        return jnp.where(flag, mine, other), jnp.where(flag, other, mine)

    def chip_states(j):
        for a in range(2):
            h = j * GROUP + 2 * core + a
            first, second = ordered(core == 0, s_all[j, 2 * core + a], x_recv[j, a].astype(F32))
            joined = dec[2 * y + 1, pl.ds(h, 1), :] * first + second
            s_chip[j, a] = joined
        y_send[j] = s_chip[j, 1 - y].astype(BF16)

    def within(b):
        cum_b = [cum_c[b * BATCH + c][:, 0:GROUP] for c in range(BATCH)]
        queries = [q_s[:, head_columns(b * BATCH + c, i)] for c, i in each]
        values = [v_s[:, head_columns(b * BATCH + c, i)] for c, i in each]
        ahead = [cum_t[pl.ds((b * BATCH + c) * GROUP + i, 1), :] for c, i in each]
        scores = [
            dot(queries[at], kc_s[b * BATCH + c, i], ((1,), (0,))) for at, (c, i) in enumerate(each)
        ]
        weights = []
        for at, (c, i) in enumerate(each):
            spread = jnp.where(s_at <= t_at, cum_b[c][:, i : i + 1] - ahead[at], -1e30)
            weights.append((scores[at] * jnp.exp(spread)).astype(BF16))
        intra = [dot(w, v, ((1,), (0,))) for w, v in zip(weights, values)]
        for at, (c, i) in enumerate(each):
            intra_s[:, head_columns(b * BATCH + c, i)] = intra[at]

    def advance(j):
        h = pl.ds(j * GROUP + 2 * core + y, 1)
        first, second = ordered(y == 0, s_chip[j, y], y_recv[j].astype(F32))
        before = z_recv[j].astype(F32)
        plane = coef[1, h, :] * first + second
        z_send[j] = (coef[2, h, :] * before + plane).astype(BF16)
        mine, other = ordered(y == 0, before, coef[0, h, :] * before + first)
        r_send[j] = other.astype(BF16)
        base[j, y] = mine.astype(BF16)

    def prefixes(j):
        for a in range(2):
            h = pl.ds(j * GROUP + 2 * core + a, 1)
            chip_base = base[j, a].astype(F32)
            chip_first = jnp.where(core == 0, s_all[j, 2 * core + a], x_recv[j, a].astype(F32))
            next_base = dec[2 * y, h, :] * chip_base + chip_first
            mine, other = ordered(core == 0, chip_base, next_base)
            pre[j, 2 * core + a] = mine.astype(BF16)
            b_send[j, a] = other.astype(BF16)

    def finish(b):
        grow = [jnp.exp(cum_c[b * BATCH + c][:, 0:GROUP]) for c in range(BATCH)]
        gain = g_ref[:, batch_columns(b)]
        queries = [q_s[:, head_columns(b * BATCH + c, i)] for c, i in each]
        intra = [intra_s[:, head_columns(b * BATCH + c, i)] for c, i in each]
        inter = [
            dot(queries[at], pre[b * BATCH + c, i], ((1,), (0,))) for at, (c, i) in enumerate(each)
        ]
        mixed = [
            intra[at] + inter[at] * grow[c][:, i : i + 1] for at, (c, i) in enumerate(each)
        ]
        scale = [lax.rsqrt(jnp.mean(m * m, axis=1, keepdims=True) + 1e-05) for m in mixed]
        result = [
            (mixed[at] * scale[at] * gain[:, at * size : (at + 1) * size]).astype(BF16)
            for at in range(len(each))
        ]
        for at, (c, i) in enumerate(each):
            out_s[:, head_columns(b * BATCH + c, i)] = result[at]

    chain_lag = jnp.minimum(2 + 2 * z, 2 * batches)
    within_lag = jnp.where(z == 0, batches + 2, jnp.where(z == 1, batches + 3, batches))
    prefix_lag = jnp.maximum(
        chain_lag + 1, jnp.where(z == 0, batches + 2, jnp.where(z == 1, 2 * batches, 0))
    )
    finish_lag = jnp.maximum(prefix_lag, within_lag) + 1

    def during(step, lag, work):
        b = step - lag

        @pl.when(jnp.logical_and(b >= 0, b < batches))
        def _():
            work(b)

    def per_chunk(work):
        def run(b):
            for c in range(BATCH):
                work(b * BATCH + c)

        return run

    def state_part(b):
        states(b)
        per_chunk(lambda j: x_copy(j).start())(b)

    def chip_part(j):
        x_copy(j).wait_recv()
        chip_states(j)
        y_copy(j).start()

    def chain_part(j):
        y_copy(j).wait_recv()

        @pl.when(has_before)
        def _():
            z_copy(j).wait_recv()

        advance(j)

        @pl.when(has_after)
        def _():
            z_copy(j).start()

        r_copy(j, y).start()

    def prefix_part(j):
        r_copy(j, 1 - y).wait_recv()
        prefixes(j)
        b_copy(j, core).start()

    def within_part(b):
        @pl.when(b == 0)
        def _():
            q_in.wait()
            small[2].wait()

        within(b)

    def finish_part(b):
        per_chunk(lambda j: b_copy(j, 1 - core).wait_recv())(b)
        finish(b)
        per_chunk(lambda j: out_copy(j).start())(b)

    def one_step(step, carry):
        during(step, 0, state_part)

        @pl.when(step == 0)
        def _():
            for off in range(1, PLANE):
                dec_copy(off, lax.rem(r - off + PLANE, PLANE)).wait_recv()
            coef[0] = dec[0] * dec[1]
            coef[1] = dec[2] * dec[3]
            coef[2] = dec[0] * dec[1] * (dec[2] * dec[3])

        during(step, 1, per_chunk(chip_part))
        during(step, chain_lag, per_chunk(chain_part))
        during(step, prefix_lag, per_chunk(prefix_part))
        during(step, within_lag, within_part)
        during(step, finish_lag, finish_part)
        return carry

    lax.fori_loop(0, 3 * batches + 3, one_step, 0)

    def drain(j, carry):
        x_copy(j).wait_send()
        y_copy(j).wait_send()
        r_copy(j, y).wait_send()
        b_copy(j, core).wait_send()

        @pl.when(has_after)
        def _():
            z_copy(j).wait_send()

        out_copy(j).wait()
        return carry

    lax.fori_loop(0, chunks, drain, 0)
    for off in range(1, PLANE):
        dec_copy(off, r).wait_send()

    @pl.when(me < n - 1)
    def _():
        halo_copy(me + 1).wait_send()


def on_device(n, queries, key_input, value_input, log_decay, conv_weight, norm_gain):
    rows, width = queries.shape
    heads = log_decay.shape[1]
    size = width // heads
    chunks = heads // GROUP
    pair = pltpu.VMEM((chunks, 2, size, size), BF16)
    one = pltpu.VMEM((chunks, size, size), BF16)
    pair_wide = pltpu.VMEM((chunks, 2, size, size), F32)
    hbm = pl.BlockSpec(memory_space=pltpu.HBM)
    dma = pltpu.SemaphoreType.DMA
    block = pltpu.VMEM((rows, width), BF16)
    arguments = (
        queries, key_input, value_input, log_decay.T, conv_weight, norm_gain.reshape(1, width)
    )
    return pl.pallas_call(
        functools.partial(kernel, n),
        out_shape=jax.ShapeDtypeStruct((rows, width), BF16),
        in_specs=[hbm] * 6,
        out_specs=pl.BlockSpec(memory_space=pl.ANY),
        scratch_shapes=[
            pltpu.VMEM((heads, rows), F32),
            pltpu.VMEM(conv_weight.shape, F32),
            pltpu.VMEM((1, width), F32),
            block, block, block, block,
            pltpu.VMEM((TAIL, width), BF16),
            pltpu.VMEM((TAIL, width // PARTS), BF16),
            pltpu.VMEM((TAIL, width // PARTS), BF16),
            pltpu.VMEM((8, width), F32),
            pltpu.VMEM((rows + 8, BATCH * GROUP * size), F32),
            pltpu.VMEM((chunks, GROUP, size, rows), BF16),
            pltpu.VMEM((rows, width), F32),
            pltpu.VMEM((chunks, rows, size), F32),
            pltpu.VMEM((heads, rows), F32),
            pltpu.VMEM((heads, rows), F32),
            pltpu.VMEM((PLANE, heads, size), F32),
            pltpu.VMEM((3, heads, size), F32),
            pltpu.VMEM((chunks, GROUP, size, size), F32),
            pltpu.VMEM((chunks, GROUP, size, size), BF16),
            pair, pair_wide, one, one, one, one, one, pair, pair,
            pltpu.VMEM((chunks, GROUP, size, size), BF16),
            dma((2, chunks // BATCH)), dma, dma, dma((3,)), dma((2,)), dma((PLANE - 1,)), dma((PLANE - 1,)),
            dma((2, chunks)), dma((2, chunks)), dma((2, chunks)), dma((2, chunks)), dma((2, chunks)),
            dma((chunks,)),
        ],
        compiler_params=pltpu.CompilerParams(
            collective_id=0, has_side_effects=True, vmem_limit_bytes=52 * 1024 * 1024
        ),
        name="decayed_attention",
    )(*(pltpu.with_memory_space_constraint(x, pltpu.HBM) for x in arguments))


def solution(mesh):
    rows = P(("groups", "ctx"), None)
    return jax.shard_map(
        functools.partial(on_device, mesh.shape["ctx"]),
        mesh=mesh,
        in_specs=(rows, rows, rows, rows, P(), P()),
        out_specs=rows,
        check_vma=False,
    )
```

```python
import functools

import jax
import jax.numpy as jnp
from jax import lax
from jax.experimental import pallas as pl
from jax.experimental.pallas import tpu as pltpu
from jax.sharding import PartitionSpec as P

MESH = pl.DeviceIdType.MESH
F32 = jnp.float32
BF16 = jnp.bfloat16
PLANE = 4
GROUP = 4
BATCH = 2
TAIL = 16
PARTS = 4


def dot(a, b, contract, precision=None):
    return lax.dot_general(
        a, b, (contract, ((), ())), preferred_element_type=F32, precision=precision
    )


def kernel(
    n, q_hbm, k_hbm, v_hbm, ld_hbm, w_hbm, g_hbm, out_hbm,
    ld_ref, w_ref, g_ref, q_s, k_s, v_s, out_s, tail, tail_out, tail_in, halo, kx, kc_s, intra_s, cum_c, cum_t, fade_t, dec, coef,
    s_all, s_low, x_recv, s_chip, y_send, y_recv, z_send, z_recv, r_send, base, b_send, pre,
    in_sem, q_sem, tail_sem, small_sem, halo_sem, dec_send_sem, dec_recv_sem, x_sem, y_sem, z_sem, r_sem, b_sem, out_sem,
):
    rows, width = q_s.shape
    heads = ld_ref.shape[0]
    size = width // heads
    chunks = heads // GROUP
    taps = w_ref.shape[0]
    cols = GROUP * size
    planes = n // PLANE

    me = lax.axis_index("ctx")
    r = lax.rem(me, PLANE)
    z = lax.div(me, PLANE)
    core = lax.rem(me, 2)
    y = lax.div(r, 2)
    sibling = me + 1 - 2 * core
    across = me + 2 - 4 * y
    has_before = z > 0
    has_after = z < planes - 1

    barrier = pltpu.get_barrier_semaphore()

    def greet(target):
        pl.semaphore_signal(barrier, inc=1, device_id={"ctx": target}, device_id_type=MESH)

    for off in range(1, PLANE):
        greet(z * PLANE + lax.rem(r + off, PLANE))
    links = (
        (has_before, me - PLANE),
        (has_after, me + PLANE),
        (jnp.logical_and(has_before, r == 0), me - 1),
        (jnp.logical_and(has_after, r == PLANE - 1), me + 1),
    )
    for there, target in links:
        @pl.when(there)
        def _(target=target):
            greet(target)

    batches = chunks // BATCH
    each = [(c, i) for c in range(BATCH) for i in range(GROUP)]

    def chunk_columns(j):
        return pl.ds(pl.multiple_of(j * cols, cols), cols)

    def batch_columns(b):
        return pl.ds(pl.multiple_of(b * BATCH * cols, BATCH * cols), BATCH * cols)

    def load(source, target, kind, j):
        here = batch_columns(j)
        return pltpu.make_async_copy(source.at[:, here], target.at[:, here], in_sem.at[kind, j])

    small = [
        pltpu.make_async_copy(source, target, small_sem.at[at])
        for at, (source, target) in enumerate(((ld_hbm, ld_ref), (w_hbm, w_ref), (g_hbm, g_ref)))
    ]
    small[0].start()
    tail_load = pltpu.make_async_copy(k_hbm.at[pl.ds(rows - TAIL, TAIL), :], tail, tail_sem)
    tail_load.start()
    small[1].start()

    def start_loads(j, carry):
        load(k_hbm, k_s, 0, j).start()
        load(v_hbm, v_s, 1, j).start()
        return carry

    lax.fori_loop(0, batches, start_loads, 0)
    q_in = pltpu.make_async_copy(q_hbm, q_s, q_sem)
    q_in.start()
    small[2].start()

    keep = taps - 1
    part = width // PARTS
    tail_load.wait()
    last = tail[...].astype(F32)[TAIL - keep : TAIL]
    packed = [last[:, p * part : (p + 1) * part] for p in range(PARTS)]
    packed.append(jnp.zeros((TAIL - PARTS * keep, part), F32))
    tail_out[...] = jnp.concatenate(packed, axis=0).astype(BF16)

    guests = PLANE - 1
    for there, _ in links:
        guests = guests + jnp.where(there, 1, 0)
    pl.semaphore_wait(barrier, guests)

    def halo_copy(target):
        return pltpu.make_async_remote_copy(
            src_ref=tail_out,
            dst_ref=tail_in,
            send_sem=halo_sem.at[0],
            recv_sem=halo_sem.at[1],
            device_id={"ctx": target},
            device_id_type=MESH,
        )

    @pl.when(me < n - 1)
    def _():
        halo_copy(me + 1).start()

    t_at = lax.broadcasted_iota(jnp.int32, (rows, rows), 0)
    s_at = lax.broadcasted_iota(jnp.int32, (rows, rows), 1)
    lower = jnp.where(s_at <= t_at, 1.0, 0.0).astype(F32)
    upper = jnp.where(t_at <= s_at, 1.0, 0.0).astype(F32)
    small[0].wait()
    log_decay = ld_ref[...]
    cum = dot(lower, log_decay, ((1,), (1,)), lax.Precision.HIGHEST)
    for c in range(chunks):
        cum_c[c, :, 0:GROUP] = cum[:, c * GROUP : (c + 1) * GROUP]
    cum_rows = dot(log_decay, upper, ((1,), (0,)), lax.Precision.HIGHEST)
    cum_t[...] = cum_rows
    dec[r] = jnp.broadcast_to(jnp.exp(cum_rows[:, rows - 1 : rows]), (heads, size))

    fade_t[...] = jnp.exp(cum_rows[:, rows - 1 : rows] - cum_rows)

    def dec_copy(off, slot):
        return pltpu.make_async_remote_copy(
            src_ref=dec.at[slot],
            dst_ref=dec.at[slot],
            send_sem=dec_send_sem.at[off - 1],
            recv_sem=dec_recv_sem.at[off - 1],
            device_id={"ctx": z * PLANE + lax.rem(r + off, PLANE)},
            device_id_type=MESH,
        )

    for off in range(1, PLANE):
        dec_copy(off, r).start()

    def x_copy(j):
        return pltpu.make_async_remote_copy(
            src_ref=s_low.at[j, pl.ds(2 * (1 - core), 2)],
            dst_ref=x_recv.at[j],
            send_sem=x_sem.at[0, j],
            recv_sem=x_sem.at[1, j],
            device_id={"ctx": sibling},
            device_id_type=MESH,
        )

    def y_copy(j):
        return pltpu.make_async_remote_copy(
            src_ref=y_send.at[j],
            dst_ref=y_recv.at[j],
            send_sem=y_sem.at[0, j],
            recv_sem=y_sem.at[1, j],
            device_id={"ctx": across},
            device_id_type=MESH,
        )

    def z_copy(j):
        return pltpu.make_async_remote_copy(
            src_ref=z_send.at[j],
            dst_ref=z_recv.at[j],
            send_sem=z_sem.at[0, j],
            recv_sem=z_sem.at[1, j],
            device_id={"ctx": me + PLANE},
            device_id_type=MESH,
        )

    def r_copy(j, owner):
        return pltpu.make_async_remote_copy(
            src_ref=r_send.at[j],
            dst_ref=base.at[j, owner],
            send_sem=r_sem.at[0, j],
            recv_sem=r_sem.at[1, j],
            device_id={"ctx": across},
            device_id_type=MESH,
        )

    def b_copy(j, owner):
        return pltpu.make_async_remote_copy(
            src_ref=b_send.at[j],
            dst_ref=pre.at[j, pl.ds(2 * owner, 2)],
            send_sem=b_sem.at[0, j],
            recv_sem=b_sem.at[1, j],
            device_id={"ctx": sibling},
            device_id_type=MESH,
        )

    def out_copy(j):
        here = chunk_columns(j)
        return pltpu.make_async_copy(out_s.at[:, here], out_hbm.at[:, here], out_sem.at[j])

    @pl.when(jnp.logical_not(has_before))
    def _():
        z_recv[...] = jnp.zeros_like(z_recv)

    small[1].wait()

    @pl.when(me == 0)
    def _():
        halo[...] = jnp.zeros_like(halo)

    @pl.when(me > 0)
    def _():
        halo_copy(me).wait_recv()
        got = tail_in[...].astype(F32)
        for p in range(PARTS):
            halo[8 - keep : 8, p * part : (p + 1) * part] = got[p * keep : (p + 1) * keep]

    def head_columns(j, i):
        return pl.ds(pl.multiple_of(j * cols + i * size, size), size)

    def states(b):
        load(k_hbm, k_s, 0, b).wait()
        load(v_hbm, v_s, 1, b).wait()
        wide = batch_columns(b)
        kx[0:8, :] = halo[:, wide]
        kx[pl.ds(8, rows), :] = k_s[:, wide].astype(F32)
        taps_b = w_ref[:, wide]
        fade = [fade_t[pl.ds((b * BATCH + c) * GROUP + i, 1), :] for c, i in each]
        values = [v_s[:, head_columns(b * BATCH + c, i)] for c, i in each]
        turned = []
        for c, i in each:
            near = slice((c * GROUP + i) * size, (c * GROUP + i + 1) * size)
            total = taps_b[0:1, near] * kx[pl.ds(8, rows), near]
            for tap in range(1, taps):
                total = total + taps_b[tap : tap + 1, near] * kx[pl.ds(8 - tap, rows), near]
            turned.append(total.astype(BF16).T)
        weighted = [(t.astype(F32) * f).astype(BF16) for t, f in zip(turned, fade)]
        state = [dot(w, v, ((1,), (0,))) for w, v in zip(weighted, values)]
        for at, (c, i) in enumerate(each):
            kc_s[b * BATCH + c, i] = turned[at]
            s_all[b * BATCH + c, i] = state[at]
            s_low[b * BATCH + c, i] = state[at].astype(BF16)

    def ordered(flag, mine, other):
        return jnp.where(flag, mine, other), jnp.where(flag, other, mine)

    def chip_states(j):
        for a in range(2):
            h = j * GROUP + 2 * core + a
            first, second = ordered(core == 0, s_all[j, 2 * core + a], x_recv[j, a].astype(F32))
            joined = dec[2 * y + 1, pl.ds(h, 1), :] * first + second
            s_chip[j, a] = joined
        y_send[j] = s_chip[j, 1 - y].astype(BF16)

    def within(b):
        cum_b = [cum_c[b * BATCH + c][:, 0:GROUP] for c in range(BATCH)]
        queries = [q_s[:, head_columns(b * BATCH + c, i)] for c, i in each]
        values = [v_s[:, head_columns(b * BATCH + c, i)] for c, i in each]
        ahead = [cum_t[pl.ds((b * BATCH + c) * GROUP + i, 1), :] for c, i in each]
        scores = [
            dot(queries[at], kc_s[b * BATCH + c, i], ((1,), (0,))) for at, (c, i) in enumerate(each)
        ]
        weights = []
        for at, (c, i) in enumerate(each):
            spread = jnp.where(s_at <= t_at, cum_b[c][:, i : i + 1] - ahead[at], -1e30)
            weights.append((scores[at] * jnp.exp(spread)).astype(BF16))
        intra = [dot(w, v, ((1,), (0,))) for w, v in zip(weights, values)]
        for at, (c, i) in enumerate(each):
            intra_s[:, head_columns(b * BATCH + c, i)] = intra[at]

    def advance(j):
        h = pl.ds(j * GROUP + 2 * core + y, 1)
        first, second = ordered(y == 0, s_chip[j, y], y_recv[j].astype(F32))
        before = z_recv[j].astype(F32)
        plane = coef[1, h, :] * first + second
        z_send[j] = (coef[2, h, :] * before + plane).astype(BF16)
        mine, other = ordered(y == 0, before, coef[0, h, :] * before + first)
        r_send[j] = other.astype(BF16)
        base[j, y] = mine.astype(BF16)

    def prefixes(j):
        for a in range(2):
            h = pl.ds(j * GROUP + 2 * core + a, 1)
            chip_base = base[j, a].astype(F32)
            chip_first = jnp.where(core == 0, s_all[j, 2 * core + a], x_recv[j, a].astype(F32))
            next_base = dec[2 * y, h, :] * chip_base + chip_first
            mine, other = ordered(core == 0, chip_base, next_base)
            pre[j, 2 * core + a] = mine.astype(BF16)
            b_send[j, a] = other.astype(BF16)

    def finish(b):
        grow = [jnp.exp(cum_c[b * BATCH + c][:, 0:GROUP]) for c in range(BATCH)]
        gain = g_ref[:, batch_columns(b)]
        queries = [q_s[:, head_columns(b * BATCH + c, i)] for c, i in each]
        intra = [intra_s[:, head_columns(b * BATCH + c, i)] for c, i in each]
        inter = [
            dot(queries[at], pre[b * BATCH + c, i], ((1,), (0,))) for at, (c, i) in enumerate(each)
        ]
        mixed = [
            intra[at] + inter[at] * grow[c][:, i : i + 1] for at, (c, i) in enumerate(each)
        ]
        scale = [lax.rsqrt(jnp.mean(m * m, axis=1, keepdims=True) + 1e-05) for m in mixed]
        result = [
            (mixed[at] * scale[at] * gain[:, at * size : (at + 1) * size]).astype(BF16)
            for at in range(len(each))
        ]
        for at, (c, i) in enumerate(each):
            out_s[:, head_columns(b * BATCH + c, i)] = result[at]

    chain_lag = jnp.where(z == 0, 3, jnp.minimum(2 + 2 * z, 2 * batches))
    within_lag = jnp.where(z == 0, batches + 2, jnp.where(z == 1, batches + 3, batches - 1))
    prefix_lag = jnp.where(z < 2, batches + 3 + z, chain_lag + 2)
    finish_lag = jnp.maximum(prefix_lag, within_lag) + 1

    def during(step, lag, work):
        b = step - lag

        @pl.when(jnp.logical_and(b >= 0, b < batches))
        def _():
            work(b)

    def per_chunk(work):
        def run(b):
            for c in range(BATCH):
                work(b * BATCH + c)

        return run

    def state_part(b):
        states(b)
        per_chunk(lambda j: x_copy(j).start())(b)

    def chip_part(j):
        x_copy(j).wait_recv()
        chip_states(j)
        y_copy(j).start()

    def chain_part(j):
        y_copy(j).wait_recv()

        @pl.when(has_before)
        def _():
            z_copy(j).wait_recv()

        advance(j)

        @pl.when(has_after)
        def _():
            z_copy(j).start()

        r_copy(j, y).start()

    def prefix_part(j):
        r_copy(j, 1 - y).wait_recv()
        prefixes(j)
        b_copy(j, core).start()

    def within_part(b):
        @pl.when(b == 0)
        def _():
            q_in.wait()
            small[2].wait()

        within(b)

    def finish_part(b):
        per_chunk(lambda j: b_copy(j, 1 - core).wait_recv())(b)
        finish(b)
        per_chunk(lambda j: out_copy(j).start())(b)

    def one_step(step, carry):
        during(step, 0, state_part)

        @pl.when(step == 1)
        def _():
            for off in range(1, PLANE):
                dec_copy(off, lax.rem(r - off + PLANE, PLANE)).wait_recv()
            coef[0] = dec[0] * dec[1]
            coef[1] = dec[2] * dec[3]
            coef[2] = dec[0] * dec[1] * (dec[2] * dec[3])

        during(step, 1, per_chunk(chip_part))
        during(step, chain_lag, per_chunk(chain_part))
        during(step, prefix_lag, per_chunk(prefix_part))
        during(step, within_lag, within_part)
        during(step, finish_lag, finish_part)
        return carry

    lax.fori_loop(0, 3 * batches + 5, one_step, 0)

    def drain(j, carry):
        x_copy(j).wait_send()
        y_copy(j).wait_send()
        r_copy(j, y).wait_send()
        b_copy(j, core).wait_send()

        @pl.when(has_after)
        def _():
            z_copy(j).wait_send()

        out_copy(j).wait()
        return carry

    lax.fori_loop(0, chunks, drain, 0)
    for off in range(1, PLANE):
        dec_copy(off, r).wait_send()

    @pl.when(me < n - 1)
    def _():
        halo_copy(me + 1).wait_send()


def on_device(n, queries, key_input, value_input, log_decay, conv_weight, norm_gain):
    rows, width = queries.shape
    heads = log_decay.shape[1]
    size = width // heads
    chunks = heads // GROUP
    pair = pltpu.VMEM((chunks, 2, size, size), BF16)
    one = pltpu.VMEM((chunks, size, size), BF16)
    pair_wide = pltpu.VMEM((chunks, 2, size, size), F32)
    hbm = pl.BlockSpec(memory_space=pltpu.HBM)
    dma = pltpu.SemaphoreType.DMA
    block = pltpu.VMEM((rows, width), BF16)
    arguments = (
        queries, key_input, value_input, log_decay.T, conv_weight, norm_gain.reshape(1, width)
    )
    return pl.pallas_call(
        functools.partial(kernel, n),
        out_shape=jax.ShapeDtypeStruct((rows, width), BF16),
        in_specs=[hbm] * 6,
        out_specs=pl.BlockSpec(memory_space=pl.ANY),
        scratch_shapes=[
            pltpu.VMEM((heads, rows), F32),
            pltpu.VMEM(conv_weight.shape, F32),
            pltpu.VMEM((1, width), F32),
            block, block, block, block,
            pltpu.VMEM((TAIL, width), BF16),
            pltpu.VMEM((TAIL, width // PARTS), BF16),
            pltpu.VMEM((TAIL, width // PARTS), BF16),
            pltpu.VMEM((8, width), F32),
            pltpu.VMEM((rows + 8, BATCH * GROUP * size), F32),
            pltpu.VMEM((chunks, GROUP, size, rows), BF16),
            pltpu.VMEM((rows, width), F32),
            pltpu.VMEM((chunks, rows, size), F32),
            pltpu.VMEM((heads, rows), F32),
            pltpu.VMEM((heads, rows), F32),
            pltpu.VMEM((PLANE, heads, size), F32),
            pltpu.VMEM((3, heads, size), F32),
            pltpu.VMEM((chunks, GROUP, size, size), F32),
            pltpu.VMEM((chunks, GROUP, size, size), BF16),
            pair, pair_wide, one, one, one, one, one, pair, pair,
            pltpu.VMEM((chunks, GROUP, size, size), BF16),
            dma((2, chunks // BATCH)), dma, dma, dma((3,)), dma((2,)), dma((PLANE - 1,)), dma((PLANE - 1,)),
            dma((2, chunks)), dma((2, chunks)), dma((2, chunks)), dma((2, chunks)), dma((2, chunks)),
            dma((chunks,)),
        ],
        compiler_params=pltpu.CompilerParams(
            collective_id=0, has_side_effects=True, vmem_limit_bytes=52 * 1024 * 1024
        ),
        name="decayed_attention",
    )(*(pltpu.with_memory_space_constraint(x, pltpu.HBM) for x in arguments))


def solution(mesh):
    rows = P(("groups", "ctx"), None)
    return jax.shard_map(
        functools.partial(on_device, mesh.shape["ctx"]),
        mesh=mesh,
        in_specs=(rows, rows, rows, rows, P(), P()),
        out_specs=rows,
        check_vma=False,
    )
```

```python
import functools

import jax
import jax.numpy as jnp
from jax import lax
from jax.experimental import pallas as pl
from jax.experimental.pallas import tpu as pltpu
from jax.sharding import PartitionSpec as P

MESH = pl.DeviceIdType.MESH
F32 = jnp.float32
BF16 = jnp.bfloat16
PLANE = 4
GROUP = 4
BATCH = 2
TAIL = 16
PARTS = 4


def dot(a, b, contract, precision=None):
    return lax.dot_general(
        a, b, (contract, ((), ())), preferred_element_type=F32, precision=precision
    )


def kernel(
    n, q_hbm, k_hbm, v_hbm, ld_hbm, w_hbm, g_hbm, out_hbm,
    ld_ref, w_ref, g_ref, q_s, k_s, v_s, out_s, tail, tail_out, tail_in, halo, kx, kc_s, intra_s, cum_c, cum_t, fade_t, dec, coef,
    s_all, s_low, x_recv, s_chip, y_send, y_recv, z_send, z_recv, r_send, base, b_send, pre,
    in_sem, q_sem, tail_sem, small_sem, halo_sem, dec_send_sem, dec_recv_sem, x_sem, y_sem, z_sem, r_sem, b_sem, out_sem,
):
    rows, width = q_s.shape
    heads = ld_ref.shape[0]
    size = width // heads
    chunks = heads // GROUP
    taps = w_ref.shape[0]
    cols = GROUP * size
    planes = n // PLANE

    me = lax.axis_index("ctx")
    r = lax.rem(me, PLANE)
    z = lax.div(me, PLANE)
    core = lax.rem(me, 2)
    y = lax.div(r, 2)
    sibling = me + 1 - 2 * core
    across = me + 2 - 4 * y
    has_before = z > 0
    has_after = z < planes - 1

    barrier = pltpu.get_barrier_semaphore()

    def greet(target):
        pl.semaphore_signal(barrier, inc=1, device_id={"ctx": target}, device_id_type=MESH)

    for off in range(1, PLANE):
        greet(z * PLANE + lax.rem(r + off, PLANE))
    links = (
        (has_before, me - PLANE),
        (has_after, me + PLANE),
        (jnp.logical_and(has_before, r == 0), me - 1),
        (jnp.logical_and(has_after, r == PLANE - 1), me + 1),
    )
    for there, target in links:
        @pl.when(there)
        def _(target=target):
            greet(target)

    batches = chunks // BATCH
    each = [(c, i) for c in range(BATCH) for i in range(GROUP)]

    def chunk_columns(j):
        return pl.ds(pl.multiple_of(j * cols, cols), cols)

    def batch_columns(b):
        return pl.ds(pl.multiple_of(b * BATCH * cols, BATCH * cols), BATCH * cols)

    def load(source, target, kind, j):
        here = batch_columns(j)
        return pltpu.make_async_copy(source.at[:, here], target.at[:, here], in_sem.at[kind, j])

    small = [
        pltpu.make_async_copy(source, target, small_sem.at[at])
        for at, (source, target) in enumerate(((ld_hbm, ld_ref), (w_hbm, w_ref), (g_hbm, g_ref)))
    ]
    small[0].start()
    tail_load = pltpu.make_async_copy(k_hbm.at[pl.ds(rows - TAIL, TAIL), :], tail, tail_sem)
    tail_load.start()
    small[1].start()

    def start_loads(j, carry):
        load(k_hbm, k_s, 0, j).start()
        load(v_hbm, v_s, 1, j).start()
        return carry

    lax.fori_loop(0, batches, start_loads, 0)
    q_in = pltpu.make_async_copy(q_hbm, q_s, q_sem)
    q_in.start()
    small[2].start()

    keep = taps - 1
    part = width // PARTS
    tail_load.wait()
    last = tail[...].astype(F32)[TAIL - keep : TAIL]
    packed = [last[:, p * part : (p + 1) * part] for p in range(PARTS)]
    packed.append(jnp.zeros((TAIL - PARTS * keep, part), F32))
    tail_out[...] = jnp.concatenate(packed, axis=0).astype(BF16)

    guests = PLANE - 1
    for there, _ in links:
        guests = guests + jnp.where(there, 1, 0)
    pl.semaphore_wait(barrier, guests)

    def halo_copy(target):
        return pltpu.make_async_remote_copy(
            src_ref=tail_out,
            dst_ref=tail_in,
            send_sem=halo_sem.at[0],
            recv_sem=halo_sem.at[1],
            device_id={"ctx": target},
            device_id_type=MESH,
        )

    @pl.when(me < n - 1)
    def _():
        halo_copy(me + 1).start()

    t_at = lax.broadcasted_iota(jnp.int32, (rows, rows), 0)
    s_at = lax.broadcasted_iota(jnp.int32, (rows, rows), 1)
    lower = jnp.where(s_at <= t_at, 1.0, 0.0).astype(F32)
    upper = jnp.where(t_at <= s_at, 1.0, 0.0).astype(F32)
    small[0].wait()
    log_decay = ld_ref[...]
    cum = dot(lower, log_decay, ((1,), (1,)), lax.Precision.HIGHEST)
    for c in range(chunks):
        cum_c[c, :, 0:GROUP] = cum[:, c * GROUP : (c + 1) * GROUP]
    cum_rows = dot(log_decay, upper, ((1,), (0,)), lax.Precision.HIGHEST)
    cum_t[...] = cum_rows
    dec[r] = jnp.broadcast_to(jnp.exp(cum_rows[:, rows - 1 : rows]), (heads, size))

    fade_t[...] = jnp.exp(cum_rows[:, rows - 1 : rows] - cum_rows)

    def dec_copy(off, slot):
        return pltpu.make_async_remote_copy(
            src_ref=dec.at[slot],
            dst_ref=dec.at[slot],
            send_sem=dec_send_sem.at[off - 1],
            recv_sem=dec_recv_sem.at[off - 1],
            device_id={"ctx": z * PLANE + lax.rem(r + off, PLANE)},
            device_id_type=MESH,
        )

    for off in range(1, PLANE):
        dec_copy(off, r).start()

    def x_copy(j):
        return pltpu.make_async_remote_copy(
            src_ref=s_low.at[j, pl.ds(2 * (1 - core), 2)],
            dst_ref=x_recv.at[j],
            send_sem=x_sem.at[0, j],
            recv_sem=x_sem.at[1, j],
            device_id={"ctx": sibling},
            device_id_type=MESH,
        )

    def y_copy(j):
        return pltpu.make_async_remote_copy(
            src_ref=y_send.at[j],
            dst_ref=y_recv.at[j],
            send_sem=y_sem.at[0, j],
            recv_sem=y_sem.at[1, j],
            device_id={"ctx": across},
            device_id_type=MESH,
        )

    def z_copy(j):
        return pltpu.make_async_remote_copy(
            src_ref=z_send.at[j],
            dst_ref=z_recv.at[j],
            send_sem=z_sem.at[0, j],
            recv_sem=z_sem.at[1, j],
            device_id={"ctx": me + PLANE},
            device_id_type=MESH,
        )

    def r_copy(j, owner):
        return pltpu.make_async_remote_copy(
            src_ref=r_send.at[j],
            dst_ref=base.at[j, owner],
            send_sem=r_sem.at[0, j],
            recv_sem=r_sem.at[1, j],
            device_id={"ctx": across},
            device_id_type=MESH,
        )

    def b_copy(j, owner):
        return pltpu.make_async_remote_copy(
            src_ref=b_send.at[j],
            dst_ref=pre.at[j, pl.ds(2 * owner, 2)],
            send_sem=b_sem.at[0, j],
            recv_sem=b_sem.at[1, j],
            device_id={"ctx": sibling},
            device_id_type=MESH,
        )

    def out_copy(j):
        here = chunk_columns(j)
        return pltpu.make_async_copy(out_s.at[:, here], out_hbm.at[:, here], out_sem.at[j])

    @pl.when(jnp.logical_not(has_before))
    def _():
        z_recv[...] = jnp.zeros_like(z_recv)

    small[1].wait()

    @pl.when(me == 0)
    def _():
        halo[...] = jnp.zeros_like(halo)

    @pl.when(me > 0)
    def _():
        halo_copy(me).wait_recv()
        got = tail_in[...].astype(F32)
        for p in range(PARTS):
            halo[8 - keep : 8, p * part : (p + 1) * part] = got[p * keep : (p + 1) * keep]

    def head_columns(j, i):
        return pl.ds(pl.multiple_of(j * cols + i * size, size), size)

    f_at = lax.broadcasted_iota(jnp.int32, (size, size), 0)
    g_at = lax.broadcasted_iota(jnp.int32, (size, size), 1)
    unit = jnp.where(f_at == g_at, 1.0, 0.0).astype(BF16)

    def states(b):
        load(k_hbm, k_s, 0, b).wait()
        load(v_hbm, v_s, 1, b).wait()
        wide = batch_columns(b)
        kx[0:8, :] = halo[:, wide]
        kx[pl.ds(8, rows), :] = k_s[:, wide].astype(F32)
        taps_b = w_ref[:, wide]
        fade = [fade_t[pl.ds((b * BATCH + c) * GROUP + i, 1), :] for c, i in each]
        values = [v_s[:, head_columns(b * BATCH + c, i)] for c, i in each]
        conv = []
        for c, i in each:
            near = slice((c * GROUP + i) * size, (c * GROUP + i + 1) * size)
            total = taps_b[0:1, near] * kx[pl.ds(8, rows), near]
            for tap in range(1, taps):
                total = total + taps_b[tap : tap + 1, near] * kx[pl.ds(8 - tap, rows), near]
            conv.append(total.astype(BF16))
        turned = [dot(unit, c, ((1,), (1,))) for c in conv]
        weighted = [(t * f).astype(BF16) for t, f in zip(turned, fade)]
        state = [dot(w, v, ((1,), (0,))) for w, v in zip(weighted, values)]
        for at, (c, i) in enumerate(each):
            kc_s[b * BATCH + c, i] = conv[at]
            s_all[b * BATCH + c, i] = state[at]
            s_low[b * BATCH + c, i] = state[at].astype(BF16)

    def ordered(flag, mine, other):
        return jnp.where(flag, mine, other), jnp.where(flag, other, mine)

    def chip_states(j):
        for a in range(2):
            h = j * GROUP + 2 * core + a
            first, second = ordered(core == 0, s_all[j, 2 * core + a], x_recv[j, a].astype(F32))
            joined = dec[2 * y + 1, pl.ds(h, 1), :] * first + second
            s_chip[j, a] = joined
        y_send[j] = s_chip[j, 1 - y].astype(BF16)

    def within(b):
        cum_b = [cum_c[b * BATCH + c][:, 0:GROUP] for c in range(BATCH)]
        queries = [q_s[:, head_columns(b * BATCH + c, i)] for c, i in each]
        values = [v_s[:, head_columns(b * BATCH + c, i)] for c, i in each]
        ahead = [cum_t[pl.ds((b * BATCH + c) * GROUP + i, 1), :] for c, i in each]
        scores = [
            dot(queries[at], kc_s[b * BATCH + c, i], ((1,), (1,))) for at, (c, i) in enumerate(each)
        ]
        weights = []
        for at, (c, i) in enumerate(each):
            spread = jnp.where(s_at <= t_at, cum_b[c][:, i : i + 1] - ahead[at], -1e30)
            weights.append((scores[at] * jnp.exp(spread)).astype(BF16))
        intra = [dot(w, v, ((1,), (0,))) for w, v in zip(weights, values)]
        for at, (c, i) in enumerate(each):
            intra_s[:, head_columns(b * BATCH + c, i)] = intra[at]

    def advance(j):
        h = pl.ds(j * GROUP + 2 * core + y, 1)
        first, second = ordered(y == 0, s_chip[j, y], y_recv[j].astype(F32))
        before = z_recv[j].astype(F32)
        plane = coef[1, h, :] * first + second
        z_send[j] = (coef[2, h, :] * before + plane).astype(BF16)
        mine, other = ordered(y == 0, before, coef[0, h, :] * before + first)
        r_send[j] = other.astype(BF16)
        base[j, y] = mine.astype(BF16)

    def prefixes(j):
        for a in range(2):
            h = pl.ds(j * GROUP + 2 * core + a, 1)
            chip_base = base[j, a].astype(F32)
            chip_first = jnp.where(core == 0, s_all[j, 2 * core + a], x_recv[j, a].astype(F32))
            next_base = dec[2 * y, h, :] * chip_base + chip_first
            mine, other = ordered(core == 0, chip_base, next_base)
            pre[j, 2 * core + a] = mine.astype(BF16)
            b_send[j, a] = other.astype(BF16)

    def finish(b):
        grow = [jnp.exp(cum_c[b * BATCH + c][:, 0:GROUP]) for c in range(BATCH)]
        gain = g_ref[:, batch_columns(b)]
        queries = [q_s[:, head_columns(b * BATCH + c, i)] for c, i in each]
        intra = [intra_s[:, head_columns(b * BATCH + c, i)] for c, i in each]
        inter = [
            dot(queries[at], pre[b * BATCH + c, i], ((1,), (0,))) for at, (c, i) in enumerate(each)
        ]
        mixed = [
            intra[at] + inter[at] * grow[c][:, i : i + 1] for at, (c, i) in enumerate(each)
        ]
        scale = [lax.rsqrt(jnp.mean(m * m, axis=1, keepdims=True) + 1e-05) for m in mixed]
        result = [
            (mixed[at] * scale[at] * gain[:, at * size : (at + 1) * size]).astype(BF16)
            for at in range(len(each))
        ]
        for at, (c, i) in enumerate(each):
            out_s[:, head_columns(b * BATCH + c, i)] = result[at]

    chain_lag = jnp.where(z == 0, 3, jnp.minimum(2 + 2 * z, 2 * batches))
    within_lag = jnp.where(z == 0, batches + 2, jnp.where(z == 1, batches + 3, batches - 1))
    prefix_lag = jnp.where(z < 2, batches + 3 + z, chain_lag + 2)
    finish_lag = jnp.maximum(prefix_lag, within_lag) + 1

    def during(step, lag, work):
        b = step - lag

        @pl.when(jnp.logical_and(b >= 0, b < batches))
        def _():
            work(b)

    def per_chunk(work):
        def run(b):
            for c in range(BATCH):
                work(b * BATCH + c)

        return run

    def state_part(b):
        states(b)
        per_chunk(lambda j: x_copy(j).start())(b)

    def chip_part(j):
        x_copy(j).wait_recv()
        chip_states(j)
        y_copy(j).start()

    def chain_part(j):
        y_copy(j).wait_recv()

        @pl.when(has_before)
        def _():
            z_copy(j).wait_recv()

        advance(j)

        @pl.when(has_after)
        def _():
            z_copy(j).start()

        r_copy(j, y).start()

    def prefix_part(j):
        r_copy(j, 1 - y).wait_recv()
        prefixes(j)
        b_copy(j, core).start()

    def within_part(b):
        @pl.when(b == 0)
        def _():
            q_in.wait()
            small[2].wait()

        within(b)

    def finish_part(b):
        per_chunk(lambda j: b_copy(j, 1 - core).wait_recv())(b)
        finish(b)
        per_chunk(lambda j: out_copy(j).start())(b)

    def one_step(step, carry):
        during(step, 0, state_part)

        @pl.when(step == 1)
        def _():
            for off in range(1, PLANE):
                dec_copy(off, lax.rem(r - off + PLANE, PLANE)).wait_recv()
            coef[0] = dec[0] * dec[1]
            coef[1] = dec[2] * dec[3]
            coef[2] = dec[0] * dec[1] * (dec[2] * dec[3])

        during(step, 1, per_chunk(chip_part))
        during(step, chain_lag, per_chunk(chain_part))
        during(step, prefix_lag, per_chunk(prefix_part))
        during(step, within_lag, within_part)
        during(step, finish_lag, finish_part)
        return carry

    lax.fori_loop(0, 3 * batches + 5, one_step, 0)

    def drain(j, carry):
        x_copy(j).wait_send()
        y_copy(j).wait_send()
        r_copy(j, y).wait_send()
        b_copy(j, core).wait_send()

        @pl.when(has_after)
        def _():
            z_copy(j).wait_send()

        out_copy(j).wait()
        return carry

    lax.fori_loop(0, chunks, drain, 0)
    for off in range(1, PLANE):
        dec_copy(off, r).wait_send()

    @pl.when(me < n - 1)
    def _():
        halo_copy(me + 1).wait_send()


def on_device(n, queries, key_input, value_input, log_decay, conv_weight, norm_gain):
    rows, width = queries.shape
    heads = log_decay.shape[1]
    size = width // heads
    chunks = heads // GROUP
    pair = pltpu.VMEM((chunks, 2, size, size), BF16)
    one = pltpu.VMEM((chunks, size, size), BF16)
    pair_wide = pltpu.VMEM((chunks, 2, size, size), F32)
    hbm = pl.BlockSpec(memory_space=pltpu.HBM)
    dma = pltpu.SemaphoreType.DMA
    block = pltpu.VMEM((rows, width), BF16)
    arguments = (
        queries, key_input, value_input, log_decay.T, conv_weight, norm_gain.reshape(1, width)
    )
    return pl.pallas_call(
        functools.partial(kernel, n),
        out_shape=jax.ShapeDtypeStruct((rows, width), BF16),
        in_specs=[hbm] * 6,
        out_specs=pl.BlockSpec(memory_space=pl.ANY),
        scratch_shapes=[
            pltpu.VMEM((heads, rows), F32),
            pltpu.VMEM(conv_weight.shape, F32),
            pltpu.VMEM((1, width), F32),
            block, block, block, block,
            pltpu.VMEM((TAIL, width), BF16),
            pltpu.VMEM((TAIL, width // PARTS), BF16),
            pltpu.VMEM((TAIL, width // PARTS), BF16),
            pltpu.VMEM((8, width), F32),
            pltpu.VMEM((rows + 8, BATCH * GROUP * size), F32),
            pltpu.VMEM((chunks, GROUP, rows, size), BF16),
            pltpu.VMEM((rows, width), F32),
            pltpu.VMEM((chunks, rows, size), F32),
            pltpu.VMEM((heads, rows), F32),
            pltpu.VMEM((heads, rows), F32),
            pltpu.VMEM((PLANE, heads, size), F32),
            pltpu.VMEM((3, heads, size), F32),
            pltpu.VMEM((chunks, GROUP, size, size), F32),
            pltpu.VMEM((chunks, GROUP, size, size), BF16),
            pair, pair_wide, one, one, one, one, one, pair, pair,
            pltpu.VMEM((chunks, GROUP, size, size), BF16),
            dma((2, chunks // BATCH)), dma, dma, dma((3,)), dma((2,)), dma((PLANE - 1,)), dma((PLANE - 1,)),
            dma((2, chunks)), dma((2, chunks)), dma((2, chunks)), dma((2, chunks)), dma((2, chunks)),
            dma((chunks,)),
        ],
        compiler_params=pltpu.CompilerParams(
            collective_id=0, has_side_effects=True, vmem_limit_bytes=52 * 1024 * 1024
        ),
        name="decayed_attention",
    )(*(pltpu.with_memory_space_constraint(x, pltpu.HBM) for x in arguments))


def solution(mesh):
    rows = P(("groups", "ctx"), None)
    return jax.shard_map(
        functools.partial(on_device, mesh.shape["ctx"]),
        mesh=mesh,
        in_specs=(rows, rows, rows, rows, P(), P()),
        out_specs=rows,
        check_vma=False,
    )
```

```python
import functools

import jax
import jax.numpy as jnp
from jax import lax
from jax.experimental import pallas as pl
from jax.experimental.pallas import tpu as pltpu
from jax.sharding import PartitionSpec as P

MESH = pl.DeviceIdType.MESH
F32 = jnp.float32
BF16 = jnp.bfloat16
PLANE = 4
GROUP = 4
BATCH = 2
TAIL = 16
PARTS = 4


def dot(a, b, contract, precision=None):
    return lax.dot_general(
        a, b, (contract, ((), ())), preferred_element_type=F32, precision=precision
    )


def kernel(
    n, q_hbm, k_hbm, v_hbm, ld_hbm, w_hbm, g_hbm, out_hbm,
    ld_ref, w_ref, g_ref, q_s, k_s, v_s, out_s, tail, tail_out, tail_in, halo, kx, kc_s, intra_s, cum_c, cum_t, fade_t, dec, coef,
    s_all, s_low, x_recv, s_chip, y_send, y_recv, z_send, z_recv, r_send, base, b_send, pre,
    in_sem, q_sem, tail_sem, small_sem, halo_sem, dec_send_sem, dec_recv_sem, x_sem, y_sem, z_sem, r_sem, b_sem, out_sem,
):
    rows, width = q_s.shape
    heads = ld_ref.shape[0]
    size = width // heads
    chunks = heads // GROUP
    taps = w_ref.shape[0]
    cols = GROUP * size
    planes = n // PLANE

    me = lax.axis_index("ctx")
    r = lax.rem(me, PLANE)
    z = lax.div(me, PLANE)
    core = lax.rem(me, 2)
    y = lax.div(r, 2)
    sibling = me + 1 - 2 * core
    across = me + 2 - 4 * y
    has_before = z > 0
    has_after = z < planes - 1

    barrier = pltpu.get_barrier_semaphore()

    def greet(target):
        pl.semaphore_signal(barrier, inc=1, device_id={"ctx": target}, device_id_type=MESH)

    for off in range(1, PLANE):
        greet(z * PLANE + lax.rem(r + off, PLANE))
    links = (
        (has_before, me - PLANE),
        (has_after, me + PLANE),
        (jnp.logical_and(has_before, r == 0), me - 1),
        (jnp.logical_and(has_after, r == PLANE - 1), me + 1),
    )
    for there, target in links:
        @pl.when(there)
        def _(target=target):
            greet(target)

    batches = chunks // BATCH
    each = [(c, i) for c in range(BATCH) for i in range(GROUP)]

    def chunk_columns(j):
        return pl.ds(pl.multiple_of(j * cols, cols), cols)

    def batch_columns(b):
        return pl.ds(pl.multiple_of(b * BATCH * cols, BATCH * cols), BATCH * cols)

    def load(source, target, kind, j):
        here = batch_columns(j)
        return pltpu.make_async_copy(source.at[:, here], target.at[:, here], in_sem.at[kind, j])

    small = [
        pltpu.make_async_copy(source, target, small_sem.at[at])
        for at, (source, target) in enumerate(((ld_hbm, ld_ref), (w_hbm, w_ref), (g_hbm, g_ref)))
    ]
    small[0].start()
    tail_load = pltpu.make_async_copy(k_hbm.at[pl.ds(rows - TAIL, TAIL), :], tail, tail_sem)
    tail_load.start()
    small[1].start()

    def start_loads(j, carry):
        load(k_hbm, k_s, 0, j).start()
        load(v_hbm, v_s, 1, j).start()
        return carry

    lax.fori_loop(0, batches, start_loads, 0)
    q_in = pltpu.make_async_copy(q_hbm, q_s, q_sem)
    q_in.start()
    small[2].start()

    keep = taps - 1
    part = width // PARTS
    tail_load.wait()
    last = tail[...].astype(F32)[TAIL - keep : TAIL]
    packed = [last[:, p * part : (p + 1) * part] for p in range(PARTS)]
    packed.append(jnp.zeros((TAIL - PARTS * keep, part), F32))
    tail_out[...] = jnp.concatenate(packed, axis=0).astype(BF16)

    guests = PLANE - 1
    for there, _ in links:
        guests = guests + jnp.where(there, 1, 0)
    pl.semaphore_wait(barrier, guests)

    def halo_copy(target):
        return pltpu.make_async_remote_copy(
            src_ref=tail_out,
            dst_ref=tail_in,
            send_sem=halo_sem.at[0],
            recv_sem=halo_sem.at[1],
            device_id={"ctx": target},
            device_id_type=MESH,
        )

    @pl.when(me < n - 1)
    def _():
        halo_copy(me + 1).start()

    t_at = lax.broadcasted_iota(jnp.int32, (rows, rows), 0)
    s_at = lax.broadcasted_iota(jnp.int32, (rows, rows), 1)
    lower = jnp.where(s_at <= t_at, 1.0, 0.0).astype(F32)
    upper = jnp.where(t_at <= s_at, 1.0, 0.0).astype(F32)
    small[0].wait()
    log_decay = ld_ref[...]
    cum = dot(lower, log_decay, ((1,), (1,)), lax.Precision.HIGHEST)
    for c in range(chunks):
        cum_c[c, :, 0:GROUP] = cum[:, c * GROUP : (c + 1) * GROUP]
    cum_rows = dot(log_decay, upper, ((1,), (0,)), lax.Precision.HIGHEST)
    cum_t[...] = cum_rows
    dec[r] = jnp.broadcast_to(jnp.exp(cum_rows[:, rows - 1 : rows]), (heads, size))

    fade_t[...] = jnp.exp(cum_rows[:, rows - 1 : rows] - cum_rows)

    def dec_copy(off, slot):
        return pltpu.make_async_remote_copy(
            src_ref=dec.at[slot],
            dst_ref=dec.at[slot],
            send_sem=dec_send_sem.at[off - 1],
            recv_sem=dec_recv_sem.at[off - 1],
            device_id={"ctx": z * PLANE + lax.rem(r + off, PLANE)},
            device_id_type=MESH,
        )

    for off in range(1, PLANE):
        dec_copy(off, r).start()

    def x_copy(j):
        return pltpu.make_async_remote_copy(
            src_ref=s_low.at[j, pl.ds(2 * (1 - core), 2)],
            dst_ref=x_recv.at[j],
            send_sem=x_sem.at[0, j],
            recv_sem=x_sem.at[1, j],
            device_id={"ctx": sibling},
            device_id_type=MESH,
        )

    def y_copy(j):
        return pltpu.make_async_remote_copy(
            src_ref=y_send.at[j],
            dst_ref=y_recv.at[j],
            send_sem=y_sem.at[0, j],
            recv_sem=y_sem.at[1, j],
            device_id={"ctx": across},
            device_id_type=MESH,
        )

    def z_copy(j):
        return pltpu.make_async_remote_copy(
            src_ref=z_send.at[j],
            dst_ref=z_recv.at[j],
            send_sem=z_sem.at[0, j],
            recv_sem=z_sem.at[1, j],
            device_id={"ctx": me + PLANE},
            device_id_type=MESH,
        )

    def r_copy(j, owner):
        return pltpu.make_async_remote_copy(
            src_ref=r_send.at[j],
            dst_ref=base.at[j, owner],
            send_sem=r_sem.at[0, j],
            recv_sem=r_sem.at[1, j],
            device_id={"ctx": across},
            device_id_type=MESH,
        )

    def b_copy(j, owner):
        return pltpu.make_async_remote_copy(
            src_ref=b_send.at[j],
            dst_ref=pre.at[j, pl.ds(2 * owner, 2)],
            send_sem=b_sem.at[0, j],
            recv_sem=b_sem.at[1, j],
            device_id={"ctx": sibling},
            device_id_type=MESH,
        )

    def out_copy(j):
        here = chunk_columns(j)
        return pltpu.make_async_copy(out_s.at[:, here], out_hbm.at[:, here], out_sem.at[j])

    @pl.when(jnp.logical_not(has_before))
    def _():
        z_recv[...] = jnp.zeros_like(z_recv)

    small[1].wait()

    @pl.when(me == 0)
    def _():
        halo[...] = jnp.zeros_like(halo)

    @pl.when(me > 0)
    def _():
        halo_copy(me).wait_recv()
        got = tail_in[...].astype(F32)
        for p in range(PARTS):
            halo[8 - keep : 8, p * part : (p + 1) * part] = got[p * keep : (p + 1) * keep]

    def head_columns(j, i):
        return pl.ds(pl.multiple_of(j * cols + i * size, size), size)

    f_at = lax.broadcasted_iota(jnp.int32, (size, size), 0)
    g_at = lax.broadcasted_iota(jnp.int32, (size, size), 1)
    unit = jnp.where(f_at == g_at, 1.0, 0.0).astype(BF16)

    def states(b):
        load(k_hbm, k_s, 0, b).wait()
        load(v_hbm, v_s, 1, b).wait()
        wide = batch_columns(b)
        kx[0:8, :] = halo[:, wide]
        kx[pl.ds(8, rows), :] = k_s[:, wide].astype(F32)
        taps_b = w_ref[:, wide]
        fade = [fade_t[pl.ds((b * BATCH + c) * GROUP + i, 1), :] for c, i in each]
        values = [v_s[:, head_columns(b * BATCH + c, i)] for c, i in each]
        conv = []
        for c, i in each:
            near = slice((c * GROUP + i) * size, (c * GROUP + i + 1) * size)
            total = taps_b[0:1, near] * kx[pl.ds(8, rows), near]
            for tap in range(1, taps):
                total = total + taps_b[tap : tap + 1, near] * kx[pl.ds(8 - tap, rows), near]
            conv.append(total.astype(BF16))
        turned = [dot(unit, c, ((1,), (1,))) for c in conv]
        weighted = [(t * f).astype(BF16) for t, f in zip(turned, fade)]
        state = [dot(w, v, ((1,), (0,))) for w, v in zip(weighted, values)]
        for at, (c, i) in enumerate(each):
            kc_s[b * BATCH + c, i] = conv[at]
            s_all[b * BATCH + c, i] = state[at]
            s_low[b * BATCH + c, i] = state[at].astype(BF16)

    def ordered(flag, mine, other):
        return jnp.where(flag, mine, other), jnp.where(flag, other, mine)

    def chip_states(j):
        for a in range(2):
            h = j * GROUP + 2 * core + a
            first, second = ordered(core == 0, s_all[j, 2 * core + a], x_recv[j, a].astype(F32))
            joined = dec[2 * y + 1, pl.ds(h, 1), :] * first + second
            s_chip[j, a] = joined
        y_send[j] = s_chip[j, 1 - y].astype(BF16)

    def within(b):
        cum_b = [cum_c[b * BATCH + c][:, 0:GROUP] for c in range(BATCH)]
        queries = [q_s[:, head_columns(b * BATCH + c, i)] for c, i in each]
        values = [v_s[:, head_columns(b * BATCH + c, i)] for c, i in each]
        ahead = [cum_t[pl.ds((b * BATCH + c) * GROUP + i, 1), :] for c, i in each]
        scores = [
            dot(queries[at], kc_s[b * BATCH + c, i], ((1,), (1,))) for at, (c, i) in enumerate(each)
        ]
        weights = []
        for at, (c, i) in enumerate(each):
            spread = jnp.where(s_at <= t_at, cum_b[c][:, i : i + 1] - ahead[at], -1e30)
            weights.append((scores[at] * jnp.exp(spread)).astype(BF16))
        intra = [dot(w, v, ((1,), (0,))) for w, v in zip(weights, values)]
        grow = [jnp.exp(c) for c in cum_b]
        grown = [
            (queries[at].astype(F32) * grow[c][:, i : i + 1]).astype(BF16)
            for at, (c, i) in enumerate(each)
        ]
        for at, (c, i) in enumerate(each):
            intra_s[:, head_columns(b * BATCH + c, i)] = intra[at]
            q_s[:, head_columns(b * BATCH + c, i)] = grown[at]

    def advance(j):
        h = pl.ds(j * GROUP + 2 * core + y, 1)
        first, second = ordered(y == 0, s_chip[j, y], y_recv[j].astype(F32))
        before = z_recv[j].astype(F32)
        plane = coef[1, h, :] * first + second
        z_send[j] = (coef[2, h, :] * before + plane).astype(BF16)

        @pl.when(has_after)
        def _():
            z_copy(j).start()

        mine, other = ordered(y == 0, before, coef[0, h, :] * before + first)
        r_send[j] = other.astype(BF16)
        base[j, y] = mine.astype(BF16)

    def prefixes(j):
        for a in range(2):
            h = pl.ds(j * GROUP + 2 * core + a, 1)
            chip_base = base[j, a].astype(F32)
            chip_first = jnp.where(core == 0, s_all[j, 2 * core + a], x_recv[j, a].astype(F32))
            next_base = dec[2 * y, h, :] * chip_base + chip_first
            mine, other = ordered(core == 0, chip_base, next_base)
            pre[j, 2 * core + a] = mine.astype(BF16)
            b_send[j, a] = other.astype(BF16)

    def finish(b):
        gain = g_ref[:, batch_columns(b)]
        queries = [q_s[:, head_columns(b * BATCH + c, i)] for c, i in each]
        intra = [intra_s[:, head_columns(b * BATCH + c, i)] for c, i in each]
        inter = [
            dot(queries[at], pre[b * BATCH + c, i], ((1,), (0,))) for at, (c, i) in enumerate(each)
        ]
        mixed = [x + y for x, y in zip(intra, inter)]
        scale = [lax.rsqrt(jnp.mean(m * m, axis=1, keepdims=True) + 1e-05) for m in mixed]
        result = [
            (mixed[at] * scale[at] * gain[:, at * size : (at + 1) * size]).astype(BF16)
            for at in range(len(each))
        ]
        for at, (c, i) in enumerate(each):
            out_s[:, head_columns(b * BATCH + c, i)] = result[at]

    chain_lag = jnp.where(z == 0, 3, jnp.minimum(2 + 2 * z, 2 * batches))
    within_lag = jnp.where(z == 0, batches + 2, jnp.where(z == 1, batches + 3, batches - 1))
    prefix_lag = jnp.where(z < 2, batches + 3 + z, chain_lag + 2)
    finish_lag = jnp.maximum(prefix_lag, within_lag) + 1

    def during(step, lag, work):
        b = step - lag

        @pl.when(jnp.logical_and(b >= 0, b < batches))
        def _():
            work(b)

    def per_chunk(work):
        def run(b):
            for c in range(BATCH):
                work(b * BATCH + c)

        return run

    def state_part(b):
        states(b)
        per_chunk(lambda j: x_copy(j).start())(b)

    def chip_part(j):
        x_copy(j).wait_recv()
        chip_states(j)
        y_copy(j).start()

    def chain_part(j):
        y_copy(j).wait_recv()

        @pl.when(has_before)
        def _():
            z_copy(j).wait_recv()

        advance(j)
        r_copy(j, y).start()

    def prefix_part(j):
        r_copy(j, 1 - y).wait_recv()
        prefixes(j)
        b_copy(j, core).start()

    def within_part(b):
        @pl.when(b == 0)
        def _():
            q_in.wait()
            small[2].wait()

        within(b)

    def finish_part(b):
        per_chunk(lambda j: b_copy(j, 1 - core).wait_recv())(b)
        finish(b)
        per_chunk(lambda j: out_copy(j).start())(b)

    def one_step(step, carry):
        during(step, 0, state_part)

        @pl.when(step == 1)
        def _():
            for off in range(1, PLANE):
                dec_copy(off, lax.rem(r - off + PLANE, PLANE)).wait_recv()
            coef[0] = dec[0] * dec[1]
            coef[1] = dec[2] * dec[3]
            coef[2] = dec[0] * dec[1] * (dec[2] * dec[3])

        during(step, 1, per_chunk(chip_part))
        during(step, chain_lag, per_chunk(chain_part))
        during(step, prefix_lag, per_chunk(prefix_part))
        during(step, within_lag, within_part)
        during(step, finish_lag, finish_part)
        return carry

    lax.fori_loop(0, 3 * batches + 5, one_step, 0)

    def drain(j, carry):
        x_copy(j).wait_send()
        y_copy(j).wait_send()
        r_copy(j, y).wait_send()
        b_copy(j, core).wait_send()

        @pl.when(has_after)
        def _():
            z_copy(j).wait_send()

        out_copy(j).wait()
        return carry

    lax.fori_loop(0, chunks, drain, 0)
    for off in range(1, PLANE):
        dec_copy(off, r).wait_send()

    @pl.when(me < n - 1)
    def _():
        halo_copy(me + 1).wait_send()


def on_device(n, queries, key_input, value_input, log_decay, conv_weight, norm_gain):
    rows, width = queries.shape
    heads = log_decay.shape[1]
    size = width // heads
    chunks = heads // GROUP
    pair = pltpu.VMEM((chunks, 2, size, size), BF16)
    one = pltpu.VMEM((chunks, size, size), BF16)
    pair_wide = pltpu.VMEM((chunks, 2, size, size), F32)
    hbm = pl.BlockSpec(memory_space=pltpu.HBM)
    dma = pltpu.SemaphoreType.DMA
    block = pltpu.VMEM((rows, width), BF16)
    arguments = (
        queries, key_input, value_input, log_decay.T, conv_weight, norm_gain.reshape(1, width)
    )
    return pl.pallas_call(
        functools.partial(kernel, n),
        out_shape=jax.ShapeDtypeStruct((rows, width), BF16),
        in_specs=[hbm] * 6,
        out_specs=pl.BlockSpec(memory_space=pl.ANY),
        scratch_shapes=[
            pltpu.VMEM((heads, rows), F32),
            pltpu.VMEM(conv_weight.shape, F32),
            pltpu.VMEM((1, width), F32),
            block, block, block, block,
            pltpu.VMEM((TAIL, width), BF16),
            pltpu.VMEM((TAIL, width // PARTS), BF16),
            pltpu.VMEM((TAIL, width // PARTS), BF16),
            pltpu.VMEM((8, width), F32),
            pltpu.VMEM((rows + 8, BATCH * GROUP * size), F32),
            pltpu.VMEM((chunks, GROUP, rows, size), BF16),
            pltpu.VMEM((rows, width), F32),
            pltpu.VMEM((chunks, rows, size), F32),
            pltpu.VMEM((heads, rows), F32),
            pltpu.VMEM((heads, rows), F32),
            pltpu.VMEM((PLANE, heads, size), F32),
            pltpu.VMEM((3, heads, size), F32),
            pltpu.VMEM((chunks, GROUP, size, size), F32),
            pltpu.VMEM((chunks, GROUP, size, size), BF16),
            pair, pair_wide, one, one, one, one, one, pair, pair,
            pltpu.VMEM((chunks, GROUP, size, size), BF16),
            dma((2, chunks // BATCH)), dma, dma, dma((3,)), dma((2,)), dma((PLANE - 1,)), dma((PLANE - 1,)),
            dma((2, chunks)), dma((2, chunks)), dma((2, chunks)), dma((2, chunks)), dma((2, chunks)),
            dma((chunks,)),
        ],
        compiler_params=pltpu.CompilerParams(
            collective_id=0, has_side_effects=True, vmem_limit_bytes=52 * 1024 * 1024
        ),
        name="decayed_attention",
    )(*(pltpu.with_memory_space_constraint(x, pltpu.HBM) for x in arguments))


def solution(mesh):
    rows = P(("groups", "ctx"), None)
    return jax.shard_map(
        functools.partial(on_device, mesh.shape["ctx"]),
        mesh=mesh,
        in_specs=(rows, rows, rows, rows, P(), P()),
        out_specs=rows,
        check_vma=False,
    )
```

```python
import functools

import jax
import jax.numpy as jnp
from jax import lax
from jax.experimental import pallas as pl
from jax.experimental.pallas import tpu as pltpu
from jax.sharding import PartitionSpec as P

MESH = pl.DeviceIdType.MESH
F32 = jnp.float32
BF16 = jnp.bfloat16
PLANE = 4
GROUP = 4
BATCH = 2
TAIL = 16
PARTS = 4


def dot(a, b, contract, precision=None):
    return lax.dot_general(
        a, b, (contract, ((), ())), preferred_element_type=F32, precision=precision
    )


def kernel(
    n, q_hbm, k_hbm, v_hbm, ld_hbm, w_hbm, g_hbm, out_hbm,
    ld_ref, w_ref, g_ref, q_s, k_s, v_s, out_s, tail, tail_out, tail_in, halo, kx, kc_s, intra_s, cum_c, cum_t, fade_t, dec, coef,
    s_all, s_low, x_recv, s_chip, y_send, y_recv, z_send, z_recv, r_send, base, b_send, pre,
    in_sem, q_sem, tail_sem, small_sem, halo_sem, dec_send_sem, dec_recv_sem, x_sem, y_sem, z_sem, r_sem, b_sem, out_sem,
):
    rows, width = q_s.shape
    heads = ld_ref.shape[0]
    size = width // heads
    chunks = heads // GROUP
    taps = w_ref.shape[0]
    cols = GROUP * size
    planes = n // PLANE

    me = lax.axis_index("ctx")
    r = lax.rem(me, PLANE)
    z = lax.div(me, PLANE)
    core = lax.rem(me, 2)
    y = lax.div(r, 2)
    sibling = me + 1 - 2 * core
    across = me + 2 - 4 * y
    has_before = z > 0
    has_after = z < planes - 1

    barrier = pltpu.get_barrier_semaphore()

    def greet(target):
        pl.semaphore_signal(barrier, inc=1, device_id={"ctx": target}, device_id_type=MESH)

    for off in range(1, PLANE):
        greet(z * PLANE + lax.rem(r + off, PLANE))
    links = (
        (has_before, me - PLANE),
        (has_after, me + PLANE),
        (jnp.logical_and(has_before, r == 0), me - 1),
        (jnp.logical_and(has_after, r == PLANE - 1), me + 1),
    )
    for there, target in links:
        @pl.when(there)
        def _(target=target):
            greet(target)

    batches = chunks // BATCH
    each = [(c, i) for c in range(BATCH) for i in range(GROUP)]

    def chunk_columns(j):
        return pl.ds(pl.multiple_of(j * cols, cols), cols)

    def batch_columns(b):
        return pl.ds(pl.multiple_of(b * BATCH * cols, BATCH * cols), BATCH * cols)

    def load(source, target, kind, j):
        here = batch_columns(j)
        return pltpu.make_async_copy(source.at[:, here], target.at[:, here], in_sem.at[kind, j])

    small = [
        pltpu.make_async_copy(source, target, small_sem.at[at])
        for at, (source, target) in enumerate(((ld_hbm, ld_ref), (w_hbm, w_ref), (g_hbm, g_ref)))
    ]
    small[0].start()
    tail_load = pltpu.make_async_copy(k_hbm.at[pl.ds(rows - TAIL, TAIL), :], tail, tail_sem)
    tail_load.start()
    small[1].start()

    def start_loads(j, carry):
        load(k_hbm, k_s, 0, j).start()
        load(v_hbm, v_s, 1, j).start()
        return carry

    lax.fori_loop(0, batches, start_loads, 0)
    q_in = pltpu.make_async_copy(q_hbm, q_s, q_sem)
    q_in.start()
    small[2].start()

    keep = taps - 1
    part = width // PARTS
    tail_load.wait()
    last = tail[...].astype(F32)[TAIL - keep : TAIL]
    packed = [last[:, p * part : (p + 1) * part] for p in range(PARTS)]
    packed.append(jnp.zeros((TAIL - PARTS * keep, part), F32))
    tail_out[...] = jnp.concatenate(packed, axis=0).astype(BF16)

    guests = PLANE - 1
    for there, _ in links:
        guests = guests + jnp.where(there, 1, 0)
    pl.semaphore_wait(barrier, guests)

    def halo_copy(target):
        return pltpu.make_async_remote_copy(
            src_ref=tail_out,
            dst_ref=tail_in,
            send_sem=halo_sem.at[0],
            recv_sem=halo_sem.at[1],
            device_id={"ctx": target},
            device_id_type=MESH,
        )

    @pl.when(me < n - 1)
    def _():
        halo_copy(me + 1).start()

    t_at = lax.broadcasted_iota(jnp.int32, (rows, rows), 0)
    s_at = lax.broadcasted_iota(jnp.int32, (rows, rows), 1)
    lower = jnp.where(s_at <= t_at, 1.0, 0.0).astype(F32)
    upper = jnp.where(t_at <= s_at, 1.0, 0.0).astype(F32)
    small[0].wait()
    log_decay = ld_ref[...]
    cum = dot(lower, log_decay, ((1,), (1,)), lax.Precision.HIGHEST)
    for c in range(chunks):
        cum_c[c, :, 0:GROUP] = cum[:, c * GROUP : (c + 1) * GROUP]
    cum_rows = dot(log_decay, upper, ((1,), (0,)), lax.Precision.HIGHEST)
    cum_t[...] = cum_rows
    dec[r] = jnp.broadcast_to(jnp.exp(cum_rows[:, rows - 1 : rows]), (heads, size))

    fade_t[...] = jnp.exp(cum_rows[:, rows - 1 : rows] - cum_rows)

    def dec_copy(off, slot):
        return pltpu.make_async_remote_copy(
            src_ref=dec.at[slot],
            dst_ref=dec.at[slot],
            send_sem=dec_send_sem.at[off - 1],
            recv_sem=dec_recv_sem.at[off - 1],
            device_id={"ctx": z * PLANE + lax.rem(r + off, PLANE)},
            device_id_type=MESH,
        )

    for off in range(1, PLANE):
        dec_copy(off, r).start()

    def span(b):
        return pl.ds(b * BATCH, BATCH)

    def x_copy(j):
        return pltpu.make_async_remote_copy(
            src_ref=s_low.at[span(j), pl.ds(2 * (1 - core), 2)],
            dst_ref=x_recv.at[span(j)],
            send_sem=x_sem.at[0, j],
            recv_sem=x_sem.at[1, j],
            device_id={"ctx": sibling},
            device_id_type=MESH,
        )

    def y_copy(j):
        return pltpu.make_async_remote_copy(
            src_ref=y_send.at[span(j)],
            dst_ref=y_recv.at[span(j)],
            send_sem=y_sem.at[0, j],
            recv_sem=y_sem.at[1, j],
            device_id={"ctx": across},
            device_id_type=MESH,
        )

    def z_copy(j):
        return pltpu.make_async_remote_copy(
            src_ref=z_send.at[span(j)],
            dst_ref=z_recv.at[span(j)],
            send_sem=z_sem.at[0, j],
            recv_sem=z_sem.at[1, j],
            device_id={"ctx": me + PLANE},
            device_id_type=MESH,
        )

    def r_copy(j, owner):
        return pltpu.make_async_remote_copy(
            src_ref=r_send.at[span(j)],
            dst_ref=base.at[span(j), owner],
            send_sem=r_sem.at[0, j],
            recv_sem=r_sem.at[1, j],
            device_id={"ctx": across},
            device_id_type=MESH,
        )

    def b_copy(j, owner):
        return pltpu.make_async_remote_copy(
            src_ref=b_send.at[span(j)],
            dst_ref=pre.at[span(j), pl.ds(2 * owner, 2)],
            send_sem=b_sem.at[0, j],
            recv_sem=b_sem.at[1, j],
            device_id={"ctx": sibling},
            device_id_type=MESH,
        )

    def out_copy(j):
        here = chunk_columns(j)
        return pltpu.make_async_copy(out_s.at[:, here], out_hbm.at[:, here], out_sem.at[j])

    @pl.when(jnp.logical_not(has_before))
    def _():
        z_recv[...] = jnp.zeros_like(z_recv)

    small[1].wait()

    @pl.when(me == 0)
    def _():
        halo[...] = jnp.zeros_like(halo)

    @pl.when(me > 0)
    def _():
        halo_copy(me).wait_recv()
        got = tail_in[...].astype(F32)
        for p in range(PARTS):
            halo[8 - keep : 8, p * part : (p + 1) * part] = got[p * keep : (p + 1) * keep]

    def head_columns(j, i):
        return pl.ds(pl.multiple_of(j * cols + i * size, size), size)

    f_at = lax.broadcasted_iota(jnp.int32, (size, size), 0)
    g_at = lax.broadcasted_iota(jnp.int32, (size, size), 1)
    unit = jnp.where(f_at == g_at, 1.0, 0.0).astype(BF16)

    def states(b):
        load(k_hbm, k_s, 0, b).wait()
        load(v_hbm, v_s, 1, b).wait()
        wide = batch_columns(b)
        kx[0:8, :] = halo[:, wide]
        kx[pl.ds(8, rows), :] = k_s[:, wide].astype(F32)
        taps_b = w_ref[:, wide]
        fade = [fade_t[pl.ds((b * BATCH + c) * GROUP + i, 1), :] for c, i in each]
        values = [v_s[:, head_columns(b * BATCH + c, i)] for c, i in each]
        conv = []
        for c, i in each:
            near = slice((c * GROUP + i) * size, (c * GROUP + i + 1) * size)
            total = taps_b[0:1, near] * kx[pl.ds(8, rows), near]
            for tap in range(1, taps):
                total = total + taps_b[tap : tap + 1, near] * kx[pl.ds(8 - tap, rows), near]
            conv.append(total.astype(BF16))
        turned = [dot(unit, c, ((1,), (1,))) for c in conv]
        weighted = [(t * f).astype(BF16) for t, f in zip(turned, fade)]
        state = [dot(w, v, ((1,), (0,))) for w, v in zip(weighted, values)]
        for at, (c, i) in enumerate(each):
            kc_s[b * BATCH + c, i] = conv[at]
            s_all[b * BATCH + c, i] = state[at]
            s_low[b * BATCH + c, i] = state[at].astype(BF16)

    def ordered(flag, mine, other):
        return jnp.where(flag, mine, other), jnp.where(flag, other, mine)

    def chip_states(j):
        for a in range(2):
            h = j * GROUP + 2 * core + a
            first, second = ordered(core == 0, s_all[j, 2 * core + a], x_recv[j, a].astype(F32))
            joined = dec[2 * y + 1, pl.ds(h, 1), :] * first + second
            s_chip[j, a] = joined
        y_send[j] = s_chip[j, 1 - y].astype(BF16)

    def within(b):
        cum_b = [cum_c[b * BATCH + c][:, 0:GROUP] for c in range(BATCH)]
        queries = [q_s[:, head_columns(b * BATCH + c, i)] for c, i in each]
        values = [v_s[:, head_columns(b * BATCH + c, i)] for c, i in each]
        ahead = [cum_t[pl.ds((b * BATCH + c) * GROUP + i, 1), :] for c, i in each]
        scores = [
            dot(queries[at], kc_s[b * BATCH + c, i], ((1,), (1,))) for at, (c, i) in enumerate(each)
        ]
        weights = []
        for at, (c, i) in enumerate(each):
            spread = jnp.where(s_at <= t_at, cum_b[c][:, i : i + 1] - ahead[at], -1e30)
            weights.append((scores[at] * jnp.exp(spread)).astype(BF16))
        intra = [dot(w, v, ((1,), (0,))) for w, v in zip(weights, values)]
        grow = [jnp.exp(c) for c in cum_b]
        grown = [
            (queries[at].astype(F32) * grow[c][:, i : i + 1]).astype(BF16)
            for at, (c, i) in enumerate(each)
        ]
        for at, (c, i) in enumerate(each):
            intra_s[:, head_columns(b * BATCH + c, i)] = intra[at]
            q_s[:, head_columns(b * BATCH + c, i)] = grown[at]

    def advance(j):
        h = pl.ds(j * GROUP + 2 * core + y, 1)
        first, second = ordered(y == 0, s_chip[j, y], y_recv[j].astype(F32))
        before = z_recv[j].astype(F32)
        plane = coef[1, h, :] * first + second
        z_send[j] = (coef[2, h, :] * before + plane).astype(BF16)
        mine, other = ordered(y == 0, before, coef[0, h, :] * before + first)
        r_send[j] = other.astype(BF16)
        base[j, y] = mine.astype(BF16)

    def prefixes(j):
        for a in range(2):
            h = pl.ds(j * GROUP + 2 * core + a, 1)
            chip_base = base[j, a].astype(F32)
            chip_first = jnp.where(core == 0, s_all[j, 2 * core + a], x_recv[j, a].astype(F32))
            next_base = dec[2 * y, h, :] * chip_base + chip_first
            mine, other = ordered(core == 0, chip_base, next_base)
            pre[j, 2 * core + a] = mine.astype(BF16)
            b_send[j, a] = other.astype(BF16)

    def finish(b):
        gain = g_ref[:, batch_columns(b)]
        queries = [q_s[:, head_columns(b * BATCH + c, i)] for c, i in each]
        intra = [intra_s[:, head_columns(b * BATCH + c, i)] for c, i in each]
        inter = [
            dot(queries[at], pre[b * BATCH + c, i], ((1,), (0,))) for at, (c, i) in enumerate(each)
        ]
        mixed = [x + y for x, y in zip(intra, inter)]
        scale = [lax.rsqrt(jnp.mean(m * m, axis=1, keepdims=True) + 1e-05) for m in mixed]
        result = [
            (mixed[at] * scale[at] * gain[:, at * size : (at + 1) * size]).astype(BF16)
            for at in range(len(each))
        ]
        for at, (c, i) in enumerate(each):
            out_s[:, head_columns(b * BATCH + c, i)] = result[at]

    chain_lag = jnp.where(z == 0, 3, jnp.minimum(2 + 2 * z, 2 * batches))
    within_lag = jnp.where(z == 0, batches + 2, jnp.where(z == 1, batches + 3, batches - 1))
    prefix_lag = jnp.where(z < 2, batches + 3 + z, chain_lag + 2)
    finish_lag = jnp.maximum(prefix_lag, within_lag) + 1

    def during(step, lag, work):
        b = step - lag

        @pl.when(jnp.logical_and(b >= 0, b < batches))
        def _():
            work(b)

    def per_chunk(work):
        def run(b):
            for c in range(BATCH):
                work(b * BATCH + c)

        return run

    def state_part(b):
        states(b)
        x_copy(b).start()

    def chip_part(b):
        x_copy(b).wait_recv()
        per_chunk(chip_states)(b)
        y_copy(b).start()

    def chain_part(b):
        y_copy(b).wait_recv()

        @pl.when(has_before)
        def _():
            z_copy(b).wait_recv()

        per_chunk(advance)(b)

        @pl.when(has_after)
        def _():
            z_copy(b).start()

        r_copy(b, y).start()

    def prefix_part(b):
        r_copy(b, 1 - y).wait_recv()
        per_chunk(prefixes)(b)
        b_copy(b, core).start()

    def within_part(b):
        @pl.when(b == 0)
        def _():
            q_in.wait()
            small[2].wait()

        within(b)

    def finish_part(b):
        b_copy(b, 1 - core).wait_recv()
        finish(b)
        per_chunk(lambda j: out_copy(j).start())(b)

    def one_step(step, carry):
        during(step, 0, state_part)

        @pl.when(step == 1)
        def _():
            for off in range(1, PLANE):
                dec_copy(off, lax.rem(r - off + PLANE, PLANE)).wait_recv()
            coef[0] = dec[0] * dec[1]
            coef[1] = dec[2] * dec[3]
            coef[2] = dec[0] * dec[1] * (dec[2] * dec[3])

        during(step, 1, chip_part)
        during(step, chain_lag, chain_part)
        during(step, prefix_lag, prefix_part)
        during(step, within_lag, within_part)
        during(step, finish_lag, finish_part)
        return carry

    lax.fori_loop(0, 3 * batches + 5, one_step, 0)

    def drain(j, carry):
        x_copy(j).wait_send()
        y_copy(j).wait_send()
        r_copy(j, y).wait_send()
        b_copy(j, core).wait_send()

        @pl.when(has_after)
        def _():
            z_copy(j).wait_send()

        per_chunk(lambda c: out_copy(c).wait())(j)
        return carry

    lax.fori_loop(0, batches, drain, 0)
    for off in range(1, PLANE):
        dec_copy(off, r).wait_send()

    @pl.when(me < n - 1)
    def _():
        halo_copy(me + 1).wait_send()


def on_device(n, queries, key_input, value_input, log_decay, conv_weight, norm_gain):
    rows, width = queries.shape
    heads = log_decay.shape[1]
    size = width // heads
    chunks = heads // GROUP
    pair = pltpu.VMEM((chunks, 2, size, size), BF16)
    one = pltpu.VMEM((chunks, size, size), BF16)
    pair_wide = pltpu.VMEM((chunks, 2, size, size), F32)
    hbm = pl.BlockSpec(memory_space=pltpu.HBM)
    dma = pltpu.SemaphoreType.DMA
    block = pltpu.VMEM((rows, width), BF16)
    arguments = (
        queries, key_input, value_input, log_decay.T, conv_weight, norm_gain.reshape(1, width)
    )
    return pl.pallas_call(
        functools.partial(kernel, n),
        out_shape=jax.ShapeDtypeStruct((rows, width), BF16),
        in_specs=[hbm] * 6,
        out_specs=pl.BlockSpec(memory_space=pl.ANY),
        scratch_shapes=[
            pltpu.VMEM((heads, rows), F32),
            pltpu.VMEM(conv_weight.shape, F32),
            pltpu.VMEM((1, width), F32),
            block, block, block, block,
            pltpu.VMEM((TAIL, width), BF16),
            pltpu.VMEM((TAIL, width // PARTS), BF16),
            pltpu.VMEM((TAIL, width // PARTS), BF16),
            pltpu.VMEM((8, width), F32),
            pltpu.VMEM((rows + 8, BATCH * GROUP * size), F32),
            pltpu.VMEM((chunks, GROUP, rows, size), BF16),
            pltpu.VMEM((rows, width), F32),
            pltpu.VMEM((chunks, rows, size), F32),
            pltpu.VMEM((heads, rows), F32),
            pltpu.VMEM((heads, rows), F32),
            pltpu.VMEM((PLANE, heads, size), F32),
            pltpu.VMEM((3, heads, size), F32),
            pltpu.VMEM((chunks, GROUP, size, size), F32),
            pltpu.VMEM((chunks, GROUP, size, size), BF16),
            pair, pair_wide, one, one, one, one, one, pair, pair,
            pltpu.VMEM((chunks, GROUP, size, size), BF16),
            dma((2, chunks // BATCH)), dma, dma, dma((3,)), dma((2,)), dma((PLANE - 1,)), dma((PLANE - 1,)),
            dma((2, chunks)), dma((2, chunks)), dma((2, chunks)), dma((2, chunks)), dma((2, chunks)),
            dma((chunks,)),
        ],
        compiler_params=pltpu.CompilerParams(
            collective_id=0, has_side_effects=True, vmem_limit_bytes=52 * 1024 * 1024
        ),
        name="decayed_attention",
    )(*(pltpu.with_memory_space_constraint(x, pltpu.HBM) for x in arguments))


def solution(mesh):
    rows = P(("groups", "ctx"), None)
    return jax.shard_map(
        functools.partial(on_device, mesh.shape["ctx"]),
        mesh=mesh,
        in_specs=(rows, rows, rows, rows, P(), P()),
        out_specs=rows,
        check_vma=False,
    )
```

```python
import functools

import jax
import jax.numpy as jnp
from jax import lax
from jax.experimental import pallas as pl
from jax.experimental.pallas import tpu as pltpu
from jax.sharding import PartitionSpec as P

MESH = pl.DeviceIdType.MESH
F32 = jnp.float32
BF16 = jnp.bfloat16
PLANE = 4
GROUP = 4
BATCH = 2
TAIL = 16
PARTS = 4


def dot(a, b, contract, precision=None):
    return lax.dot_general(
        a, b, (contract, ((), ())), preferred_element_type=F32, precision=precision
    )


def kernel(
    n, q_hbm, k_hbm, v_hbm, ld_hbm, w_hbm, g_hbm, out_hbm,
    ld_ref, w_ref, g_ref, q_s, k_s, v_s, out_s, tail, tail_out, tail_in, halo, kx, kc_s, intra_s, cum_c, cum_t, fade_t, dec, coef,
    s_all, s_low, x_recv, s_chip, y_send, y_recv, z_send, z_recv, r_send, base, b_send, pre,
    in_sem, q_sem, tail_sem, small_sem, halo_sem, dec_send_sem, dec_recv_sem, x_sem, y_sem, z_sem, r_sem, b_sem, out_sem,
):
    rows, width = q_s.shape
    heads = ld_ref.shape[0]
    size = width // heads
    chunks = heads // GROUP
    taps = w_ref.shape[0]
    cols = GROUP * size
    planes = n // PLANE

    me = lax.axis_index("ctx")
    r = lax.rem(me, PLANE)
    z = lax.div(me, PLANE)
    core = lax.rem(me, 2)
    y = lax.div(r, 2)
    sibling = me + 1 - 2 * core
    across = me + 2 - 4 * y
    has_before = z > 0
    has_after = z < planes - 1

    barrier = pltpu.get_barrier_semaphore()

    def greet(target):
        pl.semaphore_signal(barrier, inc=1, device_id={"ctx": target}, device_id_type=MESH)

    for off in range(1, PLANE):
        greet(z * PLANE + lax.rem(r + off, PLANE))
    links = (
        (has_before, me - PLANE),
        (has_after, me + PLANE),
        (jnp.logical_and(has_before, r == 0), me - 1),
        (jnp.logical_and(has_after, r == PLANE - 1), me + 1),
    )
    for there, target in links:
        @pl.when(there)
        def _(target=target):
            greet(target)

    batches = chunks // BATCH
    each = [(c, i) for c in range(BATCH) for i in range(GROUP)]

    def chunk_columns(j):
        return pl.ds(pl.multiple_of(j * cols, cols), cols)

    def batch_columns(b):
        return pl.ds(pl.multiple_of(b * BATCH * cols, BATCH * cols), BATCH * cols)

    def load(source, target, kind, j):
        here = batch_columns(j)
        return pltpu.make_async_copy(source.at[:, here], target.at[:, here], in_sem.at[kind, j])

    small = [
        pltpu.make_async_copy(source, target, small_sem.at[at])
        for at, (source, target) in enumerate(((ld_hbm, ld_ref), (w_hbm, w_ref), (g_hbm, g_ref)))
    ]
    small[0].start()
    tail_load = pltpu.make_async_copy(k_hbm.at[pl.ds(rows - TAIL, TAIL), :], tail, tail_sem)
    tail_load.start()
    small[1].start()

    def start_loads(j, carry):
        load(k_hbm, k_s, 0, j).start()
        load(v_hbm, v_s, 1, j).start()
        return carry

    lax.fori_loop(0, batches, start_loads, 0)
    q_in = pltpu.make_async_copy(q_hbm, q_s, q_sem)
    q_in.start()
    small[2].start()

    keep = taps - 1
    part = width // PARTS
    tail_load.wait()
    last = tail[...].astype(F32)[TAIL - keep : TAIL]
    packed = [last[:, p * part : (p + 1) * part] for p in range(PARTS)]
    packed.append(jnp.zeros((TAIL - PARTS * keep, part), F32))
    tail_out[...] = jnp.concatenate(packed, axis=0).astype(BF16)

    guests = PLANE - 1
    for there, _ in links:
        guests = guests + jnp.where(there, 1, 0)
    pl.semaphore_wait(barrier, guests)

    def halo_copy(target):
        return pltpu.make_async_remote_copy(
            src_ref=tail_out,
            dst_ref=tail_in,
            send_sem=halo_sem.at[0],
            recv_sem=halo_sem.at[1],
            device_id={"ctx": target},
            device_id_type=MESH,
        )

    @pl.when(me < n - 1)
    def _():
        halo_copy(me + 1).start()

    t_at = lax.broadcasted_iota(jnp.int32, (rows, rows), 0)
    s_at = lax.broadcasted_iota(jnp.int32, (rows, rows), 1)
    lower = jnp.where(s_at <= t_at, 1.0, 0.0).astype(F32)
    upper = jnp.where(t_at <= s_at, 1.0, 0.0).astype(F32)
    small[0].wait()
    log_decay = ld_ref[...]
    cum = dot(lower, log_decay, ((1,), (1,)), lax.Precision.HIGHEST)
    for c in range(chunks):
        cum_c[c, :, 0:GROUP] = cum[:, c * GROUP : (c + 1) * GROUP]
    cum_rows = dot(log_decay, upper, ((1,), (0,)), lax.Precision.HIGHEST)
    cum_t[...] = cum_rows
    dec[r] = jnp.broadcast_to(jnp.exp(cum_rows[:, rows - 1 : rows]), (heads, size))

    fade_t[...] = jnp.exp(cum_rows[:, rows - 1 : rows] - cum_rows)

    def dec_copy(off, slot):
        return pltpu.make_async_remote_copy(
            src_ref=dec.at[slot],
            dst_ref=dec.at[slot],
            send_sem=dec_send_sem.at[off - 1],
            recv_sem=dec_recv_sem.at[off - 1],
            device_id={"ctx": z * PLANE + lax.rem(r + off, PLANE)},
            device_id_type=MESH,
        )

    for off in range(1, PLANE):
        dec_copy(off, r).start()

    def x_copy(j):
        return pltpu.make_async_remote_copy(
            src_ref=s_low.at[j, pl.ds(2 * (1 - core), 2)],
            dst_ref=x_recv.at[j],
            send_sem=x_sem.at[0, j],
            recv_sem=x_sem.at[1, j],
            device_id={"ctx": sibling},
            device_id_type=MESH,
        )

    def y_copy(j):
        return pltpu.make_async_remote_copy(
            src_ref=y_send.at[j],
            dst_ref=y_recv.at[j],
            send_sem=y_sem.at[0, j],
            recv_sem=y_sem.at[1, j],
            device_id={"ctx": across},
            device_id_type=MESH,
        )

    def z_copy(j):
        return pltpu.make_async_remote_copy(
            src_ref=z_send.at[j],
            dst_ref=z_recv.at[j],
            send_sem=z_sem.at[0, j],
            recv_sem=z_sem.at[1, j],
            device_id={"ctx": me + PLANE},
            device_id_type=MESH,
        )

    def r_copy(j, owner):
        return pltpu.make_async_remote_copy(
            src_ref=r_send.at[j],
            dst_ref=base.at[j, owner],
            send_sem=r_sem.at[0, j],
            recv_sem=r_sem.at[1, j],
            device_id={"ctx": across},
            device_id_type=MESH,
        )

    def b_copy(j, owner):
        return pltpu.make_async_remote_copy(
            src_ref=b_send.at[j],
            dst_ref=pre.at[j, pl.ds(2 * owner, 2)],
            send_sem=b_sem.at[0, j],
            recv_sem=b_sem.at[1, j],
            device_id={"ctx": sibling},
            device_id_type=MESH,
        )

    def out_copy(j):
        here = chunk_columns(j)
        return pltpu.make_async_copy(out_s.at[:, here], out_hbm.at[:, here], out_sem.at[j])

    @pl.when(jnp.logical_not(has_before))
    def _():
        z_recv[...] = jnp.zeros_like(z_recv)

    small[1].wait()

    @pl.when(me == 0)
    def _():
        halo[...] = jnp.zeros_like(halo)

    @pl.when(me > 0)
    def _():
        halo_copy(me).wait_recv()
        got = tail_in[...].astype(F32)
        for p in range(PARTS):
            halo[8 - keep : 8, p * part : (p + 1) * part] = got[p * keep : (p + 1) * keep]

    def head_columns(j, i):
        return pl.ds(pl.multiple_of(j * cols + i * size, size), size)

    f_at = lax.broadcasted_iota(jnp.int32, (size, size), 0)
    g_at = lax.broadcasted_iota(jnp.int32, (size, size), 1)
    unit = jnp.where(f_at == g_at, 1.0, 0.0).astype(BF16)

    def states(b):
        load(k_hbm, k_s, 0, b).wait()
        load(v_hbm, v_s, 1, b).wait()
        wide = batch_columns(b)
        kx[0:8, :] = halo[:, wide]
        kx[pl.ds(8, rows), :] = k_s[:, wide].astype(F32)
        taps_b = w_ref[:, wide]
        fade = [fade_t[pl.ds((b * BATCH + c) * GROUP + i, 1), :] for c, i in each]
        values = [v_s[:, head_columns(b * BATCH + c, i)] for c, i in each]
        conv = []
        for c, i in each:
            near = slice((c * GROUP + i) * size, (c * GROUP + i + 1) * size)
            total = taps_b[0:1, near] * kx[pl.ds(8, rows), near]
            for tap in range(1, taps):
                total = total + taps_b[tap : tap + 1, near] * kx[pl.ds(8 - tap, rows), near]
            conv.append(total.astype(BF16))
        turned = [dot(unit, c, ((1,), (1,))) for c in conv]
        weighted = [(t * f).astype(BF16) for t, f in zip(turned, fade)]
        state = [dot(w, v, ((1,), (0,))) for w, v in zip(weighted, values)]
        for at, (c, i) in enumerate(each):
            kc_s[b * BATCH + c, i] = conv[at]
            s_all[b * BATCH + c, i] = state[at]
            s_low[b * BATCH + c, i] = state[at].astype(BF16)

    def ordered(flag, mine, other):
        return jnp.where(flag, mine, other), jnp.where(flag, other, mine)

    def chip_states(j):
        for a in range(2):
            h = j * GROUP + 2 * core + a
            first, second = ordered(core == 0, s_all[j, 2 * core + a], x_recv[j, a].astype(F32))
            joined = dec[2 * y + 1, pl.ds(h, 1), :] * first + second
            s_chip[j, a] = joined
        y_send[j] = s_chip[j, 1 - y].astype(BF16)

    def within(b):
        cum_b = [cum_c[b * BATCH + c][:, 0:GROUP] for c in range(BATCH)]
        queries = [q_s[:, head_columns(b * BATCH + c, i)] for c, i in each]
        values = [v_s[:, head_columns(b * BATCH + c, i)] for c, i in each]
        ahead = [cum_t[pl.ds((b * BATCH + c) * GROUP + i, 1), :] for c, i in each]
        scores = [
            dot(queries[at], kc_s[b * BATCH + c, i], ((1,), (1,))) for at, (c, i) in enumerate(each)
        ]
        weights = []
        for at, (c, i) in enumerate(each):
            spread = jnp.where(s_at <= t_at, cum_b[c][:, i : i + 1] - ahead[at], -1e30)
            weights.append((scores[at] * jnp.exp(spread)).astype(BF16))
        intra = [dot(w, v, ((1,), (0,))) for w, v in zip(weights, values)]
        grow = [jnp.exp(c) for c in cum_b]
        grown = [
            (queries[at].astype(F32) * grow[c][:, i : i + 1]).astype(BF16)
            for at, (c, i) in enumerate(each)
        ]
        for at, (c, i) in enumerate(each):
            intra_s[:, head_columns(b * BATCH + c, i)] = intra[at]
            q_s[:, head_columns(b * BATCH + c, i)] = grown[at]

    def advance(j):
        h = pl.ds(j * GROUP + 2 * core + y, 1)
        first, second = ordered(y == 0, s_chip[j, y], y_recv[j].astype(F32))
        before = z_recv[j].astype(F32)
        plane = coef[1, h, :] * first + second
        z_send[j] = (coef[2, h, :] * before + plane).astype(BF16)

        @pl.when(has_after)
        def _():
            z_copy(j).start()

        mine, other = ordered(y == 0, before, coef[0, h, :] * before + first)
        r_send[j] = other.astype(BF16)
        base[j, y] = mine.astype(BF16)

    def prefixes(j):
        for a in range(2):
            h = pl.ds(j * GROUP + 2 * core + a, 1)
            chip_base = base[j, a].astype(F32)
            chip_first = jnp.where(core == 0, s_all[j, 2 * core + a], x_recv[j, a].astype(F32))
            next_base = dec[2 * y, h, :] * chip_base + chip_first
            mine, other = ordered(core == 0, chip_base, next_base)
            pre[j, 2 * core + a] = mine.astype(BF16)
            b_send[j, a] = other.astype(BF16)

    def finish(b):
        gain = g_ref[:, batch_columns(b)]
        queries = [q_s[:, head_columns(b * BATCH + c, i)] for c, i in each]
        intra = [intra_s[:, head_columns(b * BATCH + c, i)] for c, i in each]
        inter = [
            dot(queries[at], pre[b * BATCH + c, i], ((1,), (0,))) for at, (c, i) in enumerate(each)
        ]
        mixed = [x + y for x, y in zip(intra, inter)]
        scale = [lax.rsqrt(jnp.mean(m * m, axis=1, keepdims=True) + 1e-05) for m in mixed]
        result = [
            (mixed[at] * scale[at] * gain[:, at * size : (at + 1) * size]).astype(BF16)
            for at in range(len(each))
        ]
        for at, (c, i) in enumerate(each):
            out_s[:, head_columns(b * BATCH + c, i)] = result[at]

    chain_lag = jnp.where(z == 0, 3, jnp.minimum(2 + 2 * z, 2 * batches))
    within_lag = jnp.where(z == 0, batches + 2, jnp.where(z == 1, batches + 3, batches - 1))
    prefix_lag = jnp.where(z < 2, batches + 3 + z, chain_lag + jnp.where(has_after, 2, 1))
    finish_lag = jnp.maximum(prefix_lag, within_lag) + 1

    def during(step, lag, work):
        b = step - lag

        @pl.when(jnp.logical_and(b >= 0, b < batches))
        def _():
            work(b)

    def per_chunk(work):
        def run(b):
            for c in range(BATCH):
                work(b * BATCH + c)

        return run

    def state_part(b):
        states(b)
        per_chunk(lambda j: x_copy(j).start())(b)

    def chip_part(j):
        x_copy(j).wait_recv()
        chip_states(j)
        y_copy(j).start()

    def chain_part(j):
        y_copy(j).wait_recv()

        @pl.when(has_before)
        def _():
            z_copy(j).wait_recv()

        advance(j)
        r_copy(j, y).start()

    def prefix_part(j):
        r_copy(j, 1 - y).wait_recv()
        prefixes(j)
        b_copy(j, core).start()

    def within_part(b):
        @pl.when(b == 0)
        def _():
            q_in.wait()
            small[2].wait()

        within(b)

    def finish_part(b):
        per_chunk(lambda j: b_copy(j, 1 - core).wait_recv())(b)
        finish(b)
        per_chunk(lambda j: out_copy(j).start())(b)

    def one_step(step, carry):
        during(step, 0, state_part)

        @pl.when(step == 1)
        def _():
            for off in range(1, PLANE):
                dec_copy(off, lax.rem(r - off + PLANE, PLANE)).wait_recv()
            coef[0] = dec[0] * dec[1]
            coef[1] = dec[2] * dec[3]
            coef[2] = dec[0] * dec[1] * (dec[2] * dec[3])

        during(step, 1, per_chunk(chip_part))
        during(step, chain_lag, per_chunk(chain_part))
        during(step, prefix_lag, per_chunk(prefix_part))
        during(step, within_lag, within_part)
        during(step, finish_lag, finish_part)
        return carry

    lax.fori_loop(0, 3 * batches + 5, one_step, 0)

    def drain(j, carry):
        x_copy(j).wait_send()
        y_copy(j).wait_send()
        r_copy(j, y).wait_send()
        b_copy(j, core).wait_send()

        @pl.when(has_after)
        def _():
            z_copy(j).wait_send()

        out_copy(j).wait()
        return carry

    lax.fori_loop(0, chunks, drain, 0)
    for off in range(1, PLANE):
        dec_copy(off, r).wait_send()

    @pl.when(me < n - 1)
    def _():
        halo_copy(me + 1).wait_send()


def on_device(n, queries, key_input, value_input, log_decay, conv_weight, norm_gain):
    rows, width = queries.shape
    heads = log_decay.shape[1]
    size = width // heads
    chunks = heads // GROUP
    pair = pltpu.VMEM((chunks, 2, size, size), BF16)
    one = pltpu.VMEM((chunks, size, size), BF16)
    pair_wide = pltpu.VMEM((chunks, 2, size, size), F32)
    hbm = pl.BlockSpec(memory_space=pltpu.HBM)
    dma = pltpu.SemaphoreType.DMA
    block = pltpu.VMEM((rows, width), BF16)
    arguments = (
        queries, key_input, value_input, log_decay.T, conv_weight, norm_gain.reshape(1, width)
    )
    return pl.pallas_call(
        functools.partial(kernel, n),
        out_shape=jax.ShapeDtypeStruct((rows, width), BF16),
        in_specs=[hbm] * 6,
        out_specs=pl.BlockSpec(memory_space=pl.ANY),
        scratch_shapes=[
            pltpu.VMEM((heads, rows), F32),
            pltpu.VMEM(conv_weight.shape, F32),
            pltpu.VMEM((1, width), F32),
            block, block, block, block,
            pltpu.VMEM((TAIL, width), BF16),
            pltpu.VMEM((TAIL, width // PARTS), BF16),
            pltpu.VMEM((TAIL, width // PARTS), BF16),
            pltpu.VMEM((8, width), F32),
            pltpu.VMEM((rows + 8, BATCH * GROUP * size), F32),
            pltpu.VMEM((chunks, GROUP, rows, size), BF16),
            pltpu.VMEM((rows, width), F32),
            pltpu.VMEM((chunks, rows, size), F32),
            pltpu.VMEM((heads, rows), F32),
            pltpu.VMEM((heads, rows), F32),
            pltpu.VMEM((PLANE, heads, size), F32),
            pltpu.VMEM((3, heads, size), F32),
            pltpu.VMEM((chunks, GROUP, size, size), F32),
            pltpu.VMEM((chunks, GROUP, size, size), BF16),
            pair, pair_wide, one, one, one, one, one, pair, pair,
            pltpu.VMEM((chunks, GROUP, size, size), BF16),
            dma((2, chunks // BATCH)), dma, dma, dma((3,)), dma((2,)), dma((PLANE - 1,)), dma((PLANE - 1,)),
            dma((2, chunks)), dma((2, chunks)), dma((2, chunks)), dma((2, chunks)), dma((2, chunks)),
            dma((chunks,)),
        ],
        compiler_params=pltpu.CompilerParams(
            collective_id=0, has_side_effects=True, vmem_limit_bytes=52 * 1024 * 1024
        ),
        name="decayed_attention",
    )(*(pltpu.with_memory_space_constraint(x, pltpu.HBM) for x in arguments))


def solution(mesh):
    rows = P(("groups", "ctx"), None)
    return jax.shard_map(
        functools.partial(on_device, mesh.shape["ctx"]),
        mesh=mesh,
        in_specs=(rows, rows, rows, rows, P(), P()),
        out_specs=rows,
        check_vma=False,
    )
```
